128 devices in a mesh: lat: 32 (over x, z, core), tp: 4 (over y).
Axes of the slice: x: 4, y: 4, z: 4, core: 2. Of those that a mesh axis runs over, the one named last changes fastest.
Arguments:
- z_clean: bfloat16 [128, 4096], P(None, 'tp'), may hold values from -6 to 6
- z_corrupt: bfloat16 [128, 4096], P(None, 'tp'), may hold values from -6 to 6
- resid_clean: bfloat16 [128, 3584], replicated, may hold values from -6 to 6
- resid_corrupt: bfloat16 [128, 3584], replicated, may hold values from -6 to 6
- w_out: bfloat16 [4096, 3584], P('tp'), may hold values from -0.09375 to 0.09375
- post_gain: float32 [3584], replicated, may hold values from 0.1 to 1.9
- w_enc: bfloat16 [3584, 131072], P(None, ('lat', 'tp')), may hold values from -0.09375 to 0.09375
- w_dec: bfloat16 [131072, 3584], P(('lat', 'tp')), may hold values from -1 to 1
- cot: bfloat16 [128, 4, 3584], replicated, may hold values from -6 to 6
- active: int32 [128, 131072], P(None, ('lat', 'tp')), may hold values 0 or 1
Outputs:
- latent_attr: float32 [128, 131072], P(None, ('lat', 'tp'))
- head_attr: float32 [128, 16], P('lat', 'tp')
The draws below stay inside these ranges and needn't reach their ends.
All inputs are finite; a program needn't handle non-finite values. No bound on the sum of `active` on one device may be relied on, other than what follows from the above.
Results may differ from the reference program's by a relative error of at most 0.0043.
Values sent between devices are 32-bit elements; how exact they have to be, the bound alone decides.
No kernel may reach another device: no remote copies, remote signals or barrier semaphores. Data moves between devices by JAX's collectives and lax.ppermute only.
A program may use at most 192 MiB of HBM per device.

```python
import jax
import jax.numpy as jnp
from jax import lax

D = 3584
HEADS = 16
HEAD_DIM = 256
LAT = 131072
STEPS = 4
TOKENS = 128


def draw_w_dec(key, part):
    key = jax.random.fold_in(key, 7)
    position = jnp.arange(LAT, dtype=jnp.float32) / (LAT - 1)
    base_draw = jax.random.normal(key, (LAT, D), jnp.float32)
    growth = 3.0 ** position / 1.7320508
    return (base_draw * growth[:, None] * D ** (-0.5)).astype(jnp.bfloat16)


def place_ends(array, own_key, smallest, top_value):
    longest = array.shape.index(max(array.shape))
    spots = []
    for shift in (0, 1):
        where = [jax.random.randint(jax.random.fold_in(own_key, axis), (), 0, length) for axis, length in enumerate(array.shape)]
        where[longest] = (where[longest] + shift) % array.shape[longest]
        spots.append(tuple(where))
    return array.at[spots[0]].set(smallest).at[spots[1]].set(top_value)


def levels(own_key, extent, split, low, high):
    factor_of, own = 1.0, jax.random.fold_in(own_key, 6)
    for axis_at, shards_of in split:
        steps = jnp.exp(jax.random.uniform(jax.random.fold_in(own, axis_at), (shards_of,), jnp.float32, low / len(split), high / len(split)))
        factor_of = factor_of * jnp.repeat(steps, extent[axis_at] // shards_of).reshape([-1 if axis == axis_at else 1 for axis in range(len(extent))])
    return factor_of


def normal_values(rng, extent, width, bound, shards=(), kind=jnp.bfloat16):
    level = levels(rng, extent, shards, -0.22, 0.18) if shards else 1.0
    values = jax.random.normal(rng, extent, jnp.float32) * width * level
    return jnp.minimum(jnp.maximum(values, -bound), bound).astype(kind)


def setup_inputs(seed: int = 0) -> dict:
    key_list = jax.random.split(jax.random.key(seed), 11)
    return {
        "z_clean": normal_values(key_list[0], (TOKENS, HEADS * HEAD_DIM), 1.0, 6.0, ((1, 4),)),
        "z_corrupt": normal_values(key_list[1], (TOKENS, HEADS * HEAD_DIM), 1.0, 6.0, ((1, 4),)),
        "resid_clean": normal_values(key_list[2], (TOKENS, D), 1.0, 6.0),
        "resid_corrupt": normal_values(key_list[3], (TOKENS, D), 1.0, 6.0),
        "w_out": normal_values(key_list[4], (HEADS * HEAD_DIM, D), (HEADS * HEAD_DIM) ** -0.5, 0.09375, ((0, 4),)),
        "post_gain": jnp.clip(1.0 + 0.18 * jax.random.normal(key_list[5], (D,), jnp.float32), 0.1, 1.9),
        "w_enc": normal_values(key_list[6], (D, LAT), D ** -0.5, 0.09375, ((1, 128),)),
        "w_dec": draw_w_dec(jax.random.fold_in(key_list[10], 71), 0),
        "cot": normal_values(key_list[8], (TOKENS, STEPS, D), 1.0, 6.0),
        "active": place_ends((jax.random.randint(key_list[9], (TOKENS, LAT), 0, 4) < 1).astype(jnp.int32), jax.random.fold_in(key_list[9], 1), 0, 1),
    }


EPSILON = 1e-06

def contract_last(left_side, right_side):
    return lax.dot_general(left_side, right_side, (((1,), (1,)), ((), ())), preferred_element_type=jnp.float32)

def interpolate(clean, corrupt, alphas):
    clean_f = clean.astype(jnp.float32)
    corrupt_f = corrupt.astype(jnp.float32)
    return corrupt_f[:, None, :] + alphas[None, :, None] * (clean_f - corrupt_f)[:, None, :]

def norm_backward(attn_out, inv_rms, grad_mid, post_gain):
    scaled = grad_mid * post_gain
    inner = lax.optimization_barrier(jnp.mean(attn_out * scaled, axis=-1, keepdims=True))
    return (inv_rms * scaled - attn_out * inv_rms ** 3 * inner).astype(jnp.bfloat16)

def reference(z_clean, z_corrupt, resid_clean, resid_corrupt, w_out, post_gain, w_enc, w_dec, cot, active):
    alphas = jnp.arange(STEPS, dtype=jnp.float32) / (STEPS - 1)
    row_count = TOKENS * STEPS
    z_mix = interpolate(z_clean, z_corrupt, alphas).astype(jnp.bfloat16).reshape(row_count, HEADS * HEAD_DIM)
    attn_out = jnp.dot(z_mix, w_out, preferred_element_type=jnp.float32)
    inv_rms = lax.rsqrt(lax.optimization_barrier(jnp.mean(attn_out * attn_out, axis=-1, keepdims=True)) + EPSILON)
    resid_mid = interpolate(resid_clean, resid_corrupt, alphas).reshape(row_count, D) + attn_out * inv_rms * post_gain
    sae_in = resid_mid.astype(jnp.bfloat16)
    pre_act = jnp.dot(sae_in, w_enc, preferred_element_type=jnp.float32).reshape(TOKENS, STEPS, LAT)
    active_mask = active.astype(jnp.float32)
    latents = pre_act * active_mask[:, None, :]
    delta_f = latents[:, STEPS - 1] - latents[:, 0]
    grad_f = contract_last(cot.reshape(row_count, D), w_dec).reshape(TOKENS, STEPS, LAT)
    raw_attr = delta_f * lax.optimization_barrier(jnp.mean(grad_f, axis=1))
    token_total = lax.optimization_barrier(jnp.sum(jnp.abs(raw_attr), axis=-1, keepdims=True))
    latent_attr = raw_attr / (token_total / LAT + EPSILON)
    grad_latent = (grad_f * active_mask[:, None, :]).reshape(row_count, LAT).astype(jnp.bfloat16)
    grad_mid = contract_last(grad_latent, w_enc)
    grad_attn = norm_backward(attn_out, inv_rms, grad_mid, post_gain)
    grad_heads = contract_last(grad_attn, w_out).reshape(TOKENS, STEPS, HEADS, HEAD_DIM)
    delta_z = (z_clean.astype(jnp.float32) - z_corrupt.astype(jnp.float32)).reshape(TOKENS, HEADS, HEAD_DIM)
    head_attr = lax.optimization_barrier(jnp.mean(delta_z * lax.optimization_barrier(jnp.mean(grad_heads, axis=1)), axis=-1))
    return (latent_attr, head_attr)
```

```python
import jax
import jax.numpy as jnp
from jax import lax
from jax.experimental import pallas as pl
from jax.experimental.pallas import tpu as pltpu
from jax.sharding import PartitionSpec as P

D = 3584
TOKENS = 128
STEPS = 4
HEAD_DIM = 256
HEADS_LOCAL = 4
LAT = 131072
LAT_LOCAL = 1024
EPSILON = 1e-06
OWN = 4
PLANE = 16
SIDE = 128
MSG = D + SIDE
RED = D + 2 * SIDE
HALF = RED // 2
ALPHAS = tuple(k / 3.0 for k in range(STEPS))
F32 = jnp.float32
BF16 = jnp.bfloat16
VMEM = pltpu.VMEM
MIB = 1024 * 1024


def lat_index(x, z, core):
    return ((x % 4) * 4 + z % 4) * 2 + core


PLANES = [[lat_index(x, z, c) for x in range(4) for z in range(4)] for c in range(2)]
CORE_SWAP = [(i, i ^ 1) for i in range(32)]


def call(kernel, name, operands, outs, scratch=(), mib=8, flops=10**6, hbm=()):
    spaces = [pltpu.HBM if i in hbm else VMEM for i in range(len(operands))]
    nbytes = sum(x.size * x.dtype.itemsize for x in operands)
    return pl.pallas_call(
        kernel,
        in_specs=[pl.BlockSpec(memory_space=s) for s in spaces],
        out_specs=[pl.BlockSpec(memory_space=VMEM)] * len(outs),
        out_shape=[VMEM(shape, dtype) for shape, dtype in outs],
        scratch_shapes=list(scratch),
        compiler_params=pltpu.CompilerParams(vmem_limit_bytes=mib * MIB),
        cost_estimate=pl.CostEstimate(flops=flops, bytes_accessed=nbytes, transcendentals=0),
        name=name,
    )(*[pltpu.with_memory_space_constraint(x, s) for x, s in zip(operands, spaces)])


def nt(a, b):
    return lax.dot_general(a, b, (((1,), (1,)), ((), ())), preferred_element_type=F32)


def nn(a, b):
    return lax.dot_general(a, b, (((1,), (0,)), ((), ())), preferred_element_type=F32)


def project_kernel(zc_ref, zn_ref, w_ref, heads_ref, part_ref, w_s, sems):
    copies = []
    for h in range(HEADS_LOCAL):
        rows = pl.ds(h * HEAD_DIM, HEAD_DIM)
        copies.append(pltpu.make_async_copy(w_ref.at[rows, :], w_s.at[rows, :], sems.at[h]))
        copies[-1].start()
    first = lax.axis_index("lat") * OWN
    row = lax.broadcasted_iota(jnp.int32, (16, TOKENS), 0)
    token = lax.broadcasted_iota(jnp.int32, (16, TOKENS), 1)
    pick_c = ((row < OWN) & (token == first + row)).astype(F32).astype(BF16)
    pick_n = ((row >= OWN) & (row < 2 * OWN) & (token == first + row - OWN)).astype(F32).astype(BF16)
    z = (nn(pick_c, zc_ref[...]) + nn(pick_n, zn_ref[...])).astype(BF16)
    for h in range(HEADS_LOCAL):
        copies[h].wait()
        cols = slice(h * HEAD_DIM, (h + 1) * HEAD_DIM)
        out = nn(z[:, cols], w_s[cols, :])[: 2 * OWN]
        heads_ref[h] = out
        if h == 0:
            part_ref[...] = out
        else:
            part_ref[...] += out


def project(z_corrupt, z_clean, w_out):
    return call(
        project_kernel,
        "project",
        (z_corrupt, z_clean, w_out),
        [((HEADS_LOCAL, 2 * OWN, D), F32), ((2 * OWN, D), F32)],
        [VMEM((1024, D), BF16), pltpu.SemaphoreType.DMA((HEADS_LOCAL,))],
        mib=12,
        flops=2 * 16 * 1024 * D,
        hbm=(2,),
    )


def grad_f_kernel(cot_ref, w_ref, out_ref, rows, acc):
    rows[...] = cot_ref[...].reshape(TOKENS * STEPS, D)
    for n in range(w_ref.shape[0] // acc.shape[0] // SIDE):
        base = n * acc.shape[0] * SIDE
        out = nt(rows[...], w_ref[base : base + acc.shape[0] * SIDE, :])
        for j in range(acc.shape[0]):
            acc[j] = out[:, j * SIDE : (j + 1) * SIDE]
            cols = slice(base + j * SIDE, base + (j + 1) * SIDE)
            for k in range(STEPS):
                out_ref[k, :, cols] = acc[j, pl.ds(k, TOKENS, stride=STEPS), :]


def grad_f(cot, w_dec):
    return call(
        grad_f_kernel,
        "grad_f",
        (cot, w_dec),
        [((STEPS, TOKENS, LAT_LOCAL), F32)],
        [VMEM((TOKENS * STEPS, D), BF16), VMEM((2, TOKENS * STEPS, SIDE), F32)],
        mib=8,
        flops=2 * 512 * 1024 * D,
    )[0]


def norm_kernel(a_ref, b_ref, c_ref, d_ref, rc_ref, rn_ref, gain_ref, attn_ref, msg_ref):
    attn = (a_ref[...] + b_ref[...]) + (c_ref[...] + d_ref[...])
    attn_ref[...] = attn
    first = lax.axis_index("lat") * OWN
    row = lax.broadcasted_iota(jnp.int32, (16, TOKENS), 0)
    token = lax.broadcasted_iota(jnp.int32, (16, TOKENS), 1)
    pick = ((row < 2 * OWN) & (token == first + row % OWN)).astype(F32).astype(BF16)
    corrupt = nn(pick, rc_ref[...])[: 2 * OWN]
    clean = nn(pick, rn_ref[...])[: 2 * OWN]
    upper = lax.broadcasted_iota(jnp.int32, (2 * OWN, D), 0) >= OWN
    resid = jnp.where(upper, corrupt + (clean - corrupt), corrupt)
    other = pltpu.roll(attn, OWN, 0)
    a_0 = jnp.where(upper, other, attn)
    delta = jnp.where(upper, attn, other) - a_0
    lane = lax.broadcasted_iota(jnp.int32, (2 * OWN, SIDE), 1)
    side = jnp.zeros((2 * OWN, SIDE), F32)
    invs = []
    for k in range(STEPS):
        a_k = a_0 + ALPHAS[k] * delta
        inv = lax.rsqrt(jnp.sum(a_k * a_k, axis=1, keepdims=True) * (1.0 / D) + EPSILON)
        invs.append(inv)
        side = jnp.where(lane == k, inv, side)
    low = lax.broadcasted_iota(jnp.int32, (2 * OWN, 1), 0) < OWN
    own_inv = jnp.where(low, invs[0], invs[3])
    sae_in = resid + attn * own_inv * gain_ref[...]
    for g in range(PLANE):
        msg_ref[g, :, :D] = sae_in
        msg_ref[g, :, D:] = side


def norm(parts, resid_corrupt, resid_clean, gain):
    return call(
        norm_kernel,
        "norm",
        (*parts, resid_corrupt, resid_clean, gain),
        [((2 * OWN, D), F32), ((PLANE, 2 * OWN, MSG), F32)],
    )


def resid_kernel(rc_ref, rn_ref, w_ref, out_ref):
    out_ref[0] = nn(rc_ref[...], w_ref[...])
    out_ref[1] = nn(rn_ref[...], w_ref[...])


def resid_project(resid_corrupt, resid_clean, w_enc):
    return call(
        resid_kernel,
        "resid_project",
        (resid_corrupt, resid_clean, w_enc),
        [((2, TOKENS, LAT_LOCAL), F32)],
        flops=2 * 256 * 1024 * D,
    )[0]


def own_kernel(x_ref, w_ref, out_ref):
    out_ref[...] = nn(x_ref[:, :, :D].reshape(TOKENS, D).astype(BF16), w_ref[...])


def own_project(x_own, w_enc):
    return call(
        own_kernel,
        "own_project",
        (x_own, w_enc),
        [((TOKENS, LAT_LOCAL), F32)],
        flops=2 * 128 * 1024 * D,
    )[0]


def upper_rows(width):
    return lax.broadcasted_iota(jnp.int32, (TOKENS, width), 0) % 8 >= OWN


def swap_rows(x):
    width = x.shape[-1]
    return pltpu.roll(x.reshape(PLANE, 8, width), OWN, 1).reshape(TOKENS, width)


def by_step(own, other, core):
    up = upper_rows(own.shape[-1])
    is_0 = core == 0
    x_0 = jnp.where(is_0, own, other)
    x_1 = jnp.where(is_0, other, own)
    return jnp.where(up, swap_rows(x_1), x_0), jnp.where(up, x_1, swap_rows(x_0))


def by_core(x, core):
    width = x.shape[-1]
    pairs = x.reshape(PLANE // 2, 2, 8, width)
    even, odd = pairs[:, 0], pairs[:, 1]
    up = lax.broadcasted_iota(jnp.int32, even.shape, 1) >= OWN
    core_0 = jnp.where(up, pltpu.roll(odd, OWN, 1), even).reshape(TOKENS // 2, width)
    core_1 = jnp.where(up, odd, pltpu.roll(even, OWN, 1)).reshape(TOKENS // 2, width)
    is_0 = core == 0
    return jnp.where(is_0, core_0, core_1), jnp.where(is_0, core_1, core_0)


def lane_fold(x):
    total = x[:, :SIDE]
    for start in range(SIDE, x.shape[1], SIDE):
        total = total + x[:, start : start + SIDE]
    return total


def latents_kernel(
    own_ref, other_ref, pre_ref, resid_ref, gf_ref, active_ref, w_ref,
    raw_ref, keep_ref, send_ref,
    pre_s, hidden_s, inv_s,
):
    core = lax.axis_index("lat") % 2
    pre_s[...] = nn(other_ref[:, :, :D].reshape(TOKENS, D).astype(BF16), w_ref[...])
    side = by_step(
        own_ref[:, :, D:].reshape(TOKENS, SIDE), other_ref[:, :, D:].reshape(TOKENS, SIDE), core
    )[0]
    for k in range(STEPS):
        inv_s[k] = jnp.broadcast_to(side[:, k : k + 1], (TOKENS, SIDE))
    for k, j in ((0, STEPS), (STEPS - 1, STEPS + 1)):
        inv_s[j] = 1.0 / inv_s[k]
    tot = jnp.zeros((TOKENS, SIDE), F32)
    s_0 = jnp.zeros((TOKENS, SIDE), F32)
    s_1 = jnp.zeros((TOKENS, SIDE), F32)
    half = TOKENS // 2
    for start in range(0, LAT_LOCAL, SIDE):
        cols = slice(start, start + SIDE)
        pre_0, pre_3 = by_step(pre_ref[:, cols], pre_s[:, cols], core)
        act = active_ref[:, cols].astype(F32)
        gf = [gf_ref[k, :, cols] for k in range(STEPS)]
        raw = act * (pre_3 - pre_0) * (((gf[0] + gf[1]) + (gf[2] + gf[3])) * 0.25)
        raw_ref[:, cols] = raw
        tot = tot + jnp.abs(raw)
        q_0 = act * (pre_0 - resid_ref[0, :, cols]) * inv_s[STEPS]
        q_d = act * (pre_3 - resid_ref[1, :, cols]) * inv_s[STEPS + 1] - q_0
        hidden = jnp.zeros((TOKENS, SIDE), F32)
        for k in range(STEPS):
            inv = inv_s[k]
            scaled = inv * gf[k]
            hidden = hidden + scaled
            term = inv * inv * scaled * (q_0 + ALPHAS[k] * q_d)
            s_0 = s_0 + term
            s_1 = s_1 + ALPHAS[k] * term
        own, other = by_core(act * hidden, core)
        hidden_s[:half, cols] = own.astype(BF16)
        hidden_s[half:, cols] = other.astype(BF16)
    grad = nt(hidden_s[...], w_ref[...])
    keep_ref[:, :D] = grad[:half]
    send_ref[:, :D] = grad[half:]
    row = lax.broadcasted_iota(jnp.int32, (TOKENS, SIDE), 0)
    lane = lax.broadcasted_iota(jnp.int32, (TOKENS, SIDE), 1)
    tot = jnp.sum(tot, axis=1, keepdims=True)
    tot_row = jnp.sum(jnp.where(row == lane, tot, 0.0), axis=0, keepdims=True)
    tot_all = jnp.broadcast_to(tot_row, (half, SIDE))
    s_0 = jnp.sum(s_0, axis=1, keepdims=True)
    s_1 = jnp.sum(s_1, axis=1, keepdims=True)
    own, other = by_core(jnp.where(lane == 0, s_0, jnp.where(lane == 1, s_1, 0.0)), core)
    keep_ref[:, D : D + SIDE] = tot_all
    send_ref[:, D : D + SIDE] = tot_all
    keep_ref[:, D + SIDE :] = own
    send_ref[:, D + SIDE :] = other


def latents(x_own, x_other, pre_own, resid, gf, active, w_enc):
    half = TOKENS // 2
    return call(
        latents_kernel,
        "latents",
        (x_own, x_other, pre_own, resid, gf, active, w_enc),
        [((TOKENS, LAT_LOCAL), F32), ((half, RED), F32), ((half, RED), F32)],
        [
            VMEM((TOKENS, LAT_LOCAL), F32),
            VMEM((TOKENS, LAT_LOCAL), BF16),
            VMEM((STEPS + 2, TOKENS, SIDE), F32),
        ],
        flops=4 * 128 * 1024 * D,
    )


def pair_kernel(a_ref, b_ref, out_ref):
    up = lax.broadcasted_iota(jnp.int32, (8, HALF), 0) >= OWN
    for g in range(PLANE // 2):
        tile = a_ref[8 * g : 8 * g + 8, :] + b_ref[8 * g : 8 * g + 8, :]
        left, right = tile[:, :HALF], tile[:, HALF:]
        out_ref[2 * g] = jnp.where(up, pltpu.roll(right, OWN, 0), left)
        out_ref[2 * g + 1] = jnp.where(up, right, pltpu.roll(left, OWN, 0))


def pair_sum(keep, received):
    return call(pair_kernel, "pair_sum", (keep, received), [((PLANE, 8, HALF), F32)])[0]


def plane_kernel(x_ref, out_ref):
    total = x_ref[0]
    for g in range(1, PLANE):
        total = total + x_ref[g]
    out_ref[...] = total


def plane_sum(x):
    return call(plane_kernel, "plane_sum", (x,), [((8, HALF), F32)])[0]


def result_kernel(
    a_ref, b_ref, c_ref, d_ref, attn_ref, heads_ref, gain_ref, raw_ref, latent_ref, head_ref
):
    total = (a_ref[...] + b_ref[...]) + (c_ref[...] + d_ref[...])
    rest = D - HALF
    g_left, g_right = total[:OWN], total[OWN:, :rest]
    tot_row = total[OWN : OWN + 1, rest : rest + SIDE]
    sums = total[OWN:, rest + SIDE :]
    s_0 = sums[:, 0:1] * (1.0 / D)
    s_1 = sums[:, 1:2] * (1.0 / D)
    head = jnp.zeros((OWN, HEADS_LOCAL), F32)
    lane = lax.broadcasted_iota(jnp.int32, (OWN, HEADS_LOCAL), 1)
    for part, cols in ((g_left, slice(0, HALF)), (g_right, slice(HALF, D))):
        a_0 = attn_ref[:OWN, cols]
        vec = gain_ref[:, cols] * part - (s_0 * a_0 + s_1 * (attn_ref[OWN:, cols] - a_0))
        for h in range(HEADS_LOCAL):
            v = heads_ref[h, OWN:, cols] - heads_ref[h, :OWN, cols]
            dots = jnp.sum(vec * v, axis=1, keepdims=True)
            head = head + jnp.where(lane == h, dots, 0.0)
    head_ref[...] = head * (1.0 / (HEAD_DIM * STEPS))
    row = lax.broadcasted_iota(jnp.int32, (TOKENS, SIDE), 0)
    col = lax.broadcasted_iota(jnp.int32, (TOKENS, SIDE), 1)
    tot = jnp.sum(jnp.where(row == col, tot_row, 0.0), axis=1, keepdims=True)
    latent_ref[...] = raw_ref[...] * (1.0 / (tot * (1.0 / LAT) + EPSILON))


def result(parts, attn, heads, gain, raw):
    return call(
        result_kernel,
        "result",
        (*parts, attn, heads, gain, raw),
        [((TOKENS, LAT_LOCAL), F32), ((OWN, HEADS_LOCAL), F32)],
    )


def over_tp(x):
    others = [lax.ppermute(x, "tp", [(i, (i + d) % 4) for i in range(4)]) for d in (1, 3, 2)]
    return [x] + others


def body(
    z_clean, z_corrupt, resid_clean, resid_corrupt, w_out, post_gain, w_enc, w_dec, cot, active
):
    gain = post_gain.reshape(1, D)
    heads, part = project(z_corrupt, z_clean, w_out)
    parts = over_tp(part)
    resid = resid_project(resid_corrupt, resid_clean, w_enc)
    parts, resid = lax.optimization_barrier((parts, resid))
    attn, msg = norm(parts, resid_corrupt, resid_clean, gain)
    x_own = lax.all_to_all(msg, "lat", 0, 0, axis_index_groups=PLANES)
    x_other = lax.ppermute(x_own, "lat", CORE_SWAP)
    gf = grad_f(cot, w_dec)
    pre_own = own_project(x_own, w_enc)
    raw, keep, send = latents(x_own, x_other, pre_own, resid, gf, active, w_enc)
    received = lax.ppermute(send, "lat", CORE_SWAP)
    shares = pair_sum(keep, received)
    shares = lax.all_to_all(shares, "lat", 0, 0, axis_index_groups=PLANES)
    shares = over_tp(plane_sum(shares))
    return tuple(result(shares, attn, heads, gain, raw))


def solution(mesh):
    placed = (
        P(None, "tp"),
        P(None, "tp"),
        P(),
        P(),
        P("tp", None),
        P(),
        P(None, ("lat", "tp")),
        P(("lat", "tp"), None),
        P(),
        P(None, ("lat", "tp")),
    )
    return jax.shard_map(
        body,
        mesh=mesh,
        in_specs=placed,
        out_specs=(P(None, ("lat", "tp")), P("lat", "tp")),
        check_vma=False,
    )
```

```python
import jax
import jax.numpy as jnp
from jax import lax
from jax.experimental import pallas as pl
from jax.experimental.pallas import tpu as pltpu
from jax.sharding import PartitionSpec as P

D = 3584
TOKENS = 128
STEPS = 4
HEAD_DIM = 256
HEADS_LOCAL = 4
LAT = 131072
LAT_LOCAL = 1024
EPSILON = 1e-06
OWN = 4
PLANE = 16
SIDE = 128
MSG = D + SIDE
RED = D + 2 * SIDE
HALF = RED // 2
ALPHAS = tuple(k / 3.0 for k in range(STEPS))
F32 = jnp.float32
BF16 = jnp.bfloat16
VMEM = pltpu.VMEM
MIB = 1024 * 1024


def lat_index(x, z, core):
    return ((x % 4) * 4 + z % 4) * 2 + core


def shift(stage, d):
    pairs = []
    for x in range(4):
        for z in range(4):
            for core in range(2):
                along_x = (stage == 0) == (core == 0)
                to = (x + d, z) if along_x else (x, z + d)
                pairs.append((lat_index(x, z, core), lat_index(*to, core)))
    return pairs


CORE_SWAP = [(i, i ^ 1) for i in range(32)]


def place():
    index = lax.axis_index("lat")
    return index // 8, (index // 2) % 4, index % 2


def call(kernel, name, operands, outs, scratch=(), mib=8, flops=10**6, hbm=(), final=False):
    spaces = [pltpu.HBM if i in hbm else VMEM for i in range(len(operands))]
    nbytes = sum(x.size * x.dtype.itemsize for x in operands)
    return pl.pallas_call(
        kernel,
        in_specs=[pl.BlockSpec(memory_space=s) for s in spaces],
        out_specs=[pl.BlockSpec(memory_space=VMEM)] * len(outs),
        out_shape=[(jax.ShapeDtypeStruct if final else VMEM)(shape, dtype) for shape, dtype in outs],
        scratch_shapes=list(scratch),
        compiler_params=pltpu.CompilerParams(vmem_limit_bytes=mib * MIB),
        cost_estimate=pl.CostEstimate(flops=flops, bytes_accessed=nbytes, transcendentals=0),
        name=name,
    )(*[pltpu.with_memory_space_constraint(x, s) for x, s in zip(operands, spaces)])


def nt(a, b):
    return lax.dot_general(a, b, (((1,), (1,)), ((), ())), preferred_element_type=F32)


def nn(a, b):
    return lax.dot_general(a, b, (((1,), (0,)), ((), ())), preferred_element_type=F32)


def project_kernel(zc_ref, zn_ref, w_ref, heads_ref, part_ref, z_s, w_s, z_sems, sems):
    index = lax.axis_index("lat")
    block = pl.ds(pl.multiple_of((index // 4) * 16, 16), 16)
    z_copies = [
        pltpu.make_async_copy(ref.at[block, :], z_s.at[i], z_sems.at[i])
        for i, ref in enumerate((zc_ref, zn_ref))
    ]
    for copy in z_copies:
        copy.start()
    copies = []
    for h in range(HEADS_LOCAL):
        rows = pl.ds(h * HEAD_DIM, HEAD_DIM)
        copies.append(pltpu.make_async_copy(w_ref.at[rows, :], w_s.at[rows, :], sems.at[h]))
        copies[-1].start()
    first = (index % 4) * OWN
    row = lax.broadcasted_iota(jnp.int32, (16, 16), 0)
    token = lax.broadcasted_iota(jnp.int32, (16, 16), 1)
    pick_c = ((row < OWN) & (token == first + row)).astype(F32).astype(BF16)
    pick_n = ((row >= OWN) & (row < 2 * OWN) & (token == first + row - OWN)).astype(F32).astype(BF16)
    for copy in z_copies:
        copy.wait()
    z = (nn(pick_c, z_s[0]) + nn(pick_n, z_s[1])).astype(BF16)
    for h in range(HEADS_LOCAL):
        copies[h].wait()
        cols = slice(h * HEAD_DIM, (h + 1) * HEAD_DIM)
        out = nn(z[:, cols], w_s[cols, :])[: 2 * OWN]
        heads_ref[h] = out
        if h == 0:
            part_ref[...] = out
        else:
            part_ref[...] += out


def project(z_corrupt, z_clean, w_out):
    return call(
        project_kernel,
        "project",
        (z_corrupt, z_clean, w_out),
        [((HEADS_LOCAL, 2 * OWN, D), F32), ((2 * OWN, D), F32)],
        [
            VMEM((2, 16, 1024), BF16),
            VMEM((1024, D), BF16),
            pltpu.SemaphoreType.DMA((2,)),
            pltpu.SemaphoreType.DMA((HEADS_LOCAL,)),
        ],
        mib=12,
        flops=2 * 16 * 1024 * D,
        hbm=(0, 1, 2),
    )


def grad_f_kernel(cot_ref, w_ref, out_ref, rows, acc):
    rows[...] = cot_ref[...].reshape(TOKENS * STEPS, D)
    for n in range(w_ref.shape[0] // acc.shape[0] // SIDE):
        base = n * acc.shape[0] * SIDE
        out = nt(rows[...], w_ref[base : base + acc.shape[0] * SIDE, :])
        for j in range(acc.shape[0]):
            acc[j] = out[:, j * SIDE : (j + 1) * SIDE]
            cols = slice(base + j * SIDE, base + (j + 1) * SIDE)
            for k in range(STEPS):
                out_ref[k, :, cols] = acc[j, pl.ds(k, TOKENS, stride=STEPS), :]


def grad_f(cot, w_dec):
    return call(
        grad_f_kernel,
        "grad_f",
        (cot, w_dec),
        [((STEPS, TOKENS, LAT_LOCAL), F32)],
        [VMEM((TOKENS * STEPS, D), BF16), VMEM((2, TOKENS * STEPS, SIDE), F32)],
        mib=8,
        flops=2 * 512 * 1024 * D,
    )[0]


def norm_kernel(a_ref, b_ref, c_ref, d_ref, rc_ref, rn_ref, gain_ref, attn_ref, msg_ref):
    attn = (a_ref[...] + b_ref[...]) + (c_ref[...] + d_ref[...])
    attn_ref[...] = attn
    first = lax.axis_index("lat") * OWN
    row = lax.broadcasted_iota(jnp.int32, (16, TOKENS), 0)
    token = lax.broadcasted_iota(jnp.int32, (16, TOKENS), 1)
    pick = ((row < 2 * OWN) & (token == first + row % OWN)).astype(F32).astype(BF16)
    corrupt = nn(pick, rc_ref[...])[: 2 * OWN]
    clean = nn(pick, rn_ref[...])[: 2 * OWN]
    upper = lax.broadcasted_iota(jnp.int32, (2 * OWN, D), 0) >= OWN
    resid = jnp.where(upper, corrupt + (clean - corrupt), corrupt)
    other = pltpu.roll(attn, OWN, 0)
    a_0 = jnp.where(upper, other, attn)
    delta = jnp.where(upper, attn, other) - a_0
    lane = lax.broadcasted_iota(jnp.int32, (2 * OWN, SIDE), 1)
    side = jnp.zeros((2 * OWN, SIDE), F32)
    invs = []
    for k in range(STEPS):
        a_k = a_0 + ALPHAS[k] * delta
        inv = lax.rsqrt(jnp.sum(a_k * a_k, axis=1, keepdims=True) * (1.0 / D) + EPSILON)
        invs.append(inv)
        side = jnp.where(lane == k, inv, side)
    low = lax.broadcasted_iota(jnp.int32, (2 * OWN, 1), 0) < OWN
    own_inv = jnp.where(low, invs[0], invs[3])
    sae_in = resid + attn * own_inv * gain_ref[...]
    msg_ref[:, :D] = sae_in
    msg_ref[:, D:] = side


def norm(parts, resid_corrupt, resid_clean, gain):
    return call(
        norm_kernel,
        "norm",
        (*parts, resid_corrupt, resid_clean, gain),
        [((2 * OWN, D), F32), ((2 * OWN, MSG), F32)],
    )


def line_kernel(a_ref, b_ref, c_ref, d_ref, out_ref):
    for d, ref in enumerate((a_ref, b_ref, c_ref, d_ref)):
        out_ref[d] = ref[...]


def line(parts):
    return call(line_kernel, "line", parts, [((4, 2 * OWN, MSG), F32)])[0]


def assemble(refs, core, out):
    x, z, _ = place()
    for e, ref in enumerate(refs):
        for d in range(4):
            from_x = (x + 4 - jnp.where(core == 0, d, e)) % 4
            from_z = (z + 4 - jnp.where(core == 0, e, d)) % 4
            out[from_x * 4 + from_z] = ref[d]


def resid_kernel(rc_ref, rn_ref, w_ref, out_ref):
    out_ref[0] = nn(rc_ref[...], w_ref[...])
    out_ref[1] = nn(rn_ref[...], w_ref[...])


def resid_project(resid_corrupt, resid_clean, w_enc):
    return call(
        resid_kernel,
        "resid_project",
        (resid_corrupt, resid_clean, w_enc),
        [((2, TOKENS, LAT_LOCAL), F32)],
        flops=2 * 256 * 1024 * D,
    )[0]


def own_kernel(a_ref, b_ref, c_ref, d_ref, w_ref, out_ref, side_ref, rows):
    assemble((a_ref, b_ref, c_ref, d_ref), place()[2], rows)
    side_ref[...] = rows[:, :, D:]
    out_ref[...] = nn(rows[:, :, :D].reshape(TOKENS, D).astype(BF16), w_ref[...])


def own_project(blocks, w_enc):
    return call(
        own_kernel,
        "own_project",
        (*blocks, w_enc),
        [((TOKENS, LAT_LOCAL), F32), ((PLANE, 2 * OWN, SIDE), F32)],
        [VMEM((PLANE, 2 * OWN, MSG), F32)],
        flops=2 * 128 * 1024 * D,
    )


def upper_rows(width):
    return lax.broadcasted_iota(jnp.int32, (TOKENS, width), 0) % 8 >= OWN


def swap_rows(x):
    width = x.shape[-1]
    return pltpu.roll(x.reshape(PLANE, 8, width), OWN, 1).reshape(TOKENS, width)


def by_step(own, other, core):
    up = upper_rows(own.shape[-1])
    is_0 = core == 0
    x_0 = jnp.where(is_0, own, other)
    x_1 = jnp.where(is_0, other, own)
    return jnp.where(up, swap_rows(x_1), x_0), jnp.where(up, x_1, swap_rows(x_0))


def by_core(x, core):
    width = x.shape[-1]
    pairs = x.reshape(PLANE // 2, 2, 8, width)
    even, odd = pairs[:, 0], pairs[:, 1]
    up = lax.broadcasted_iota(jnp.int32, even.shape, 1) >= OWN
    core_0 = jnp.where(up, pltpu.roll(odd, OWN, 1), even).reshape(TOKENS // 2, width)
    core_1 = jnp.where(up, odd, pltpu.roll(even, OWN, 1)).reshape(TOKENS // 2, width)
    is_0 = core == 0
    return jnp.where(is_0, core_0, core_1), jnp.where(is_0, core_1, core_0)


def lane_fold(x):
    total = x[:, :SIDE]
    for start in range(SIDE, x.shape[1], SIDE):
        total = total + x[:, start : start + SIDE]
    return total


def latents_kernel(
    a_ref, b_ref, c_ref, d_ref, side_ref, pre_ref, resid_ref, gf_ref, active_ref, w_ref,
    raw_ref, keep_ref, send_ref,
    other, pre_s, hidden_s, inv_s,
):
    core = place()[2]
    assemble((a_ref, b_ref, c_ref, d_ref), 1 - core, other)
    pre_s[...] = nn(other[:, :, :D].reshape(TOKENS, D).astype(BF16), w_ref[...])
    side = by_step(
        side_ref[...].reshape(TOKENS, SIDE), other[:, :, D:].reshape(TOKENS, SIDE), core
    )[0]
    for k in range(STEPS):
        inv_s[k] = jnp.broadcast_to(side[:, k : k + 1], (TOKENS, SIDE))
    for k, j in ((0, STEPS), (STEPS - 1, STEPS + 1)):
        inv_s[j] = 1.0 / inv_s[k]
    tot = jnp.zeros((TOKENS, SIDE), F32)
    s_0 = jnp.zeros((TOKENS, SIDE), F32)
    s_1 = jnp.zeros((TOKENS, SIDE), F32)
    half = TOKENS // 2
    for start in range(0, LAT_LOCAL, SIDE):
        cols = slice(start, start + SIDE)
        pre_0, pre_3 = by_step(pre_ref[:, cols], pre_s[:, cols], core)
        act = active_ref[:, cols].astype(F32)
        gf = [gf_ref[k, :, cols] for k in range(STEPS)]
        raw = act * (pre_3 - pre_0) * (((gf[0] + gf[1]) + (gf[2] + gf[3])) * 0.25)
        raw_ref[:, cols] = raw
        tot = tot + jnp.abs(raw)
        q_0 = act * (pre_0 - resid_ref[0, :, cols]) * inv_s[STEPS]
        q_d = act * (pre_3 - resid_ref[1, :, cols]) * inv_s[STEPS + 1] - q_0
        hidden = jnp.zeros((TOKENS, SIDE), F32)
        for k in range(STEPS):
            inv = inv_s[k]
            scaled = inv * gf[k]
            hidden = hidden + scaled
            term = inv * inv * scaled * (q_0 + ALPHAS[k] * q_d)
            s_0 = s_0 + term
            s_1 = s_1 + ALPHAS[k] * term
        first, second = by_core(act * hidden, core)
        hidden_s[:half, cols] = first.astype(BF16)
        hidden_s[half:, cols] = second.astype(BF16)
    grad = nt(hidden_s[...], w_ref[...])
    keep_ref[:, :D] = grad[:half]
    send_ref[:, :D] = grad[half:]
    row = lax.broadcasted_iota(jnp.int32, (TOKENS, SIDE), 0)
    lane = lax.broadcasted_iota(jnp.int32, (TOKENS, SIDE), 1)
    tot = jnp.sum(tot, axis=1, keepdims=True)
    tot_row = jnp.sum(jnp.where(row == lane, tot, 0.0), axis=0, keepdims=True)
    tot_all = jnp.broadcast_to(tot_row, (half, SIDE))
    s_0 = jnp.sum(s_0, axis=1, keepdims=True)
    s_1 = jnp.sum(s_1, axis=1, keepdims=True)
    first, second = by_core(jnp.where(lane == 0, s_0, jnp.where(lane == 1, s_1, 0.0)), core)
    keep_ref[:, D : D + SIDE] = tot_all
    send_ref[:, D : D + SIDE] = tot_all
    keep_ref[:, D + SIDE :] = first
    send_ref[:, D + SIDE :] = second


def latents(others, side, pre_own, resid, gf, active, w_enc):
    half = TOKENS // 2
    return call(
        latents_kernel,
        "latents",
        (*others, side, pre_own, resid, gf, active, w_enc),
        [((TOKENS, LAT_LOCAL), F32), ((half, RED), F32), ((half, RED), F32)],
        [
            VMEM((PLANE, 2 * OWN, MSG), F32),
            VMEM((TOKENS, LAT_LOCAL), F32),
            VMEM((TOKENS, LAT_LOCAL), BF16),
            VMEM((STEPS + 2, TOKENS, SIDE), F32),
        ],
        flops=4 * 128 * 1024 * D,
    )


def pair_kernel(a_ref, b_ref, p0_ref, p1_ref, p2_ref, p3_ref, packed):
    up = lax.broadcasted_iota(jnp.int32, (8, HALF), 0) >= OWN
    for g in range(PLANE // 2):
        tile = a_ref[8 * g : 8 * g + 8, :] + b_ref[8 * g : 8 * g + 8, :]
        left, right = tile[:, :HALF], tile[:, HALF:]
        packed[2 * g] = jnp.where(up, pltpu.roll(right, OWN, 0), left)
        packed[2 * g + 1] = jnp.where(up, right, pltpu.roll(left, OWN, 0))
    x, z, core = place()
    for d, ref in enumerate((p0_ref, p1_ref, p2_ref, p3_ref)):
        for b in range(4):
            to_x = jnp.where(core == 0, (x + d) % 4, b)
            to_z = jnp.where(core == 0, b, (z + d) % 4)
            ref[b] = packed[to_x * 4 + to_z]


def pair_sum(keep, received):
    return call(
        pair_kernel,
        "pair_sum",
        (keep, received),
        [((4, 8, HALF), F32)] * 4,
        [VMEM((PLANE, 8, HALF), F32)],
    )


def line_sum_kernel(a_ref, b_ref, c_ref, d_ref, p0_ref, p1_ref, p2_ref, p3_ref, total):
    total[...] = (a_ref[...] + b_ref[...]) + (c_ref[...] + d_ref[...])
    x, z, core = place()
    own = jnp.where(core == 0, z, x)
    for e, ref in enumerate((p0_ref, p1_ref, p2_ref, p3_ref)):
        ref[...] = total[(own + e) % 4]


def line_sum(parts):
    return call(
        line_sum_kernel, "line_sum", parts, [((8, HALF), F32)] * 4, [VMEM((4, 8, HALF), F32)]
    )


def plane_kernel(a_ref, b_ref, c_ref, d_ref, out_ref):
    out_ref[...] = (a_ref[...] + b_ref[...]) + (c_ref[...] + d_ref[...])


def plane_sum(parts):
    return call(plane_kernel, "plane_sum", parts, [((8, HALF), F32)])[0]


def result_kernel(
    a_ref, b_ref, c_ref, d_ref, attn_ref, heads_ref, gain_ref, raw_ref, latent_ref, head_ref
):
    total = (a_ref[...] + b_ref[...]) + (c_ref[...] + d_ref[...])
    rest = D - HALF
    g_left, g_right = total[:OWN], total[OWN:, :rest]
    tot_row = total[OWN : OWN + 1, rest : rest + SIDE]
    sums = total[OWN:, rest + SIDE :]
    s_0 = sums[:, 0:1] * (1.0 / D)
    s_1 = sums[:, 1:2] * (1.0 / D)
    head = jnp.zeros((OWN, HEADS_LOCAL), F32)
    lane = lax.broadcasted_iota(jnp.int32, (OWN, HEADS_LOCAL), 1)
    for part, cols in ((g_left, slice(0, HALF)), (g_right, slice(HALF, D))):
        a_0 = attn_ref[:OWN, cols]
        vec = gain_ref[:, cols] * part - (s_0 * a_0 + s_1 * (attn_ref[OWN:, cols] - a_0))
        for h in range(HEADS_LOCAL):
            v = heads_ref[h, OWN:, cols] - heads_ref[h, :OWN, cols]
            dots = jnp.sum(vec * v, axis=1, keepdims=True)
            head = head + jnp.where(lane == h, dots, 0.0)
    head_ref[...] = head * (1.0 / (HEAD_DIM * STEPS))
    row = lax.broadcasted_iota(jnp.int32, (TOKENS, SIDE), 0)
    col = lax.broadcasted_iota(jnp.int32, (TOKENS, SIDE), 1)
    tot = jnp.sum(jnp.where(row == col, tot_row, 0.0), axis=1, keepdims=True)
    latent_ref[...] = raw_ref[...] * (1.0 / (tot * (1.0 / LAT) + EPSILON))


def result(parts, attn, heads, gain, raw):
    return call(
        result_kernel,
        "result",
        (*parts, attn, heads, gain, raw),
        [((TOKENS, LAT_LOCAL), F32), ((OWN, HEADS_LOCAL), F32)],
        final=True,
    )


def over_tp(x):
    others = [lax.ppermute(x, "tp", [(i, (i + d) % 4) for i in range(4)]) for d in (1, 3, 2)]
    return [x] + others


def send(x, stage, d):
    return lax.ppermute(x, "lat", shift(stage, d))


def swap(x):
    return lax.ppermute(x, "lat", CORE_SWAP)


def body(
    z_clean, z_corrupt, resid_clean, resid_corrupt, w_out, post_gain, w_enc, w_dec, cot, active
):
    heads, part = project(z_corrupt, z_clean, w_out)
    part, post_gain, resid_clean, resid_corrupt, w_enc, w_dec, cot, active = lax.optimization_barrier(
        (part, post_gain, resid_clean, resid_corrupt, w_enc, w_dec, cot, active)
    )
    gain = post_gain.reshape(1, D)
    resid = resid_project(resid_corrupt, resid_clean, w_enc)
    *parts, resid = lax.optimization_barrier((*over_tp(part), resid))
    attn, msg = norm(parts, resid_corrupt, resid_clean, gain)
    gf = grad_f(cot, w_dec)
    *parts, gf = lax.optimization_barrier((msg, *[send(msg, 0, d) for d in (1, 2, 3)], gf))
    block = line(parts)
    blocks = [block] + [send(block, 1, e) for e in (1, 2, 3)]
    others = [swap(b) for b in blocks]
    pre_own, side = own_project(blocks, w_enc)
    raw, keep, give = latents(others, side, pre_own, resid, gf, active, w_enc)
    parts = pair_sum(keep, swap(give))
    parts = line_sum([parts[0]] + [send(parts[d], 0, d) for d in (1, 2, 3)])
    total = plane_sum([parts[0]] + [send(parts[e], 1, e) for e in (1, 2, 3)])
    return tuple(result(over_tp(total), attn, heads, gain, raw))


def solution(mesh):
    placed = (
        P(None, "tp"),
        P(None, "tp"),
        P(),
        P(),
        P("tp", None),
        P(),
        P(None, ("lat", "tp")),
        P(("lat", "tp"), None),
        P(),
        P(None, ("lat", "tp")),
    )
    return jax.shard_map(
        body,
        mesh=mesh,
        in_specs=placed,
        out_specs=(P(None, ("lat", "tp")), P("lat", "tp")),
        check_vma=False,
    )
```

```python
import jax
import jax.numpy as jnp
from jax import lax
from jax.experimental import pallas as pl
from jax.experimental.pallas import tpu as pltpu
from jax.sharding import PartitionSpec as P

D = 3584
TOKENS = 128
STEPS = 4
HEAD_DIM = 256
HEADS_LOCAL = 4
LAT = 131072
LAT_LOCAL = 1024
EPSILON = 1e-06
OWN = 4
PLANE = 16
SIDE = 128
MSG = D + SIDE
RED = D + 2 * SIDE
HALF = RED // 2
ALPHAS = tuple(k / 3.0 for k in range(STEPS))
F32 = jnp.float32
BF16 = jnp.bfloat16
VMEM = pltpu.VMEM
MIB = 1024 * 1024


def lat_index(x, z, core):
    return ((x % 4) * 4 + z % 4) * 2 + core


def shift(stage, d):
    pairs = []
    for x in range(4):
        for z in range(4):
            for core in range(2):
                along_x = (stage == 0) == (core == 0)
                to = (x + d, z) if along_x else (x, z + d)
                pairs.append((lat_index(x, z, core), lat_index(*to, core)))
    return pairs


CORE_SWAP = [(i, i ^ 1) for i in range(32)]


def place():
    index = lax.axis_index("lat")
    return index // 8, (index // 2) % 4, index % 2


def call(kernel, name, operands, outs, scratch=(), mib=8, flops=10**6, hbm=(), final=False):
    spaces = [pltpu.HBM if i in hbm else VMEM for i in range(len(operands))]
    nbytes = sum(x.size * x.dtype.itemsize for x in operands)
    return pl.pallas_call(
        kernel,
        in_specs=[pl.BlockSpec(memory_space=s) for s in spaces],
        out_specs=[pl.BlockSpec(memory_space=VMEM)] * len(outs),
        out_shape=[(jax.ShapeDtypeStruct if final else VMEM)(shape, dtype) for shape, dtype in outs],
        scratch_shapes=list(scratch),
        compiler_params=pltpu.CompilerParams(vmem_limit_bytes=mib * MIB),
        cost_estimate=pl.CostEstimate(flops=flops, bytes_accessed=nbytes, transcendentals=0),
        name=name,
    )(*[pltpu.with_memory_space_constraint(x, s) for x, s in zip(operands, spaces)])


def nt(a, b):
    return lax.dot_general(a, b, (((1,), (1,)), ((), ())), preferred_element_type=F32)


def nn(a, b):
    return lax.dot_general(a, b, (((1,), (0,)), ((), ())), preferred_element_type=F32)


def project_kernel(zc_ref, zn_ref, w_ref, heads_ref, part_ref, z_s, w_s, z_sems, sems):
    index = lax.axis_index("lat")
    block = pl.ds(pl.multiple_of((index // 4) * 16, 16), 16)
    z_copies = [
        pltpu.make_async_copy(ref.at[block, :], z_s.at[i], z_sems.at[i])
        for i, ref in enumerate((zc_ref, zn_ref))
    ]
    for copy in z_copies:
        copy.start()
    copies = []
    for h in range(HEADS_LOCAL):
        rows = pl.ds(h * HEAD_DIM, HEAD_DIM)
        copies.append(pltpu.make_async_copy(w_ref.at[rows, :], w_s.at[rows, :], sems.at[h]))
        copies[-1].start()
    first = (index % 4) * OWN
    row = lax.broadcasted_iota(jnp.int32, (16, 16), 0)
    token = lax.broadcasted_iota(jnp.int32, (16, 16), 1)
    pick_c = ((row < OWN) & (token == first + row)).astype(F32).astype(BF16)
    pick_n = ((row >= OWN) & (row < 2 * OWN) & (token == first + row - OWN)).astype(F32).astype(BF16)
    for copy in z_copies:
        copy.wait()
    z = (nn(pick_c, z_s[0]) + nn(pick_n, z_s[1])).astype(BF16)
    for h in range(HEADS_LOCAL):
        copies[h].wait()
        cols = slice(h * HEAD_DIM, (h + 1) * HEAD_DIM)
        out = nn(z[:, cols], w_s[cols, :])[: 2 * OWN]
        heads_ref[h] = out
        if h == 0:
            part_ref[...] = out
        else:
            part_ref[...] += out


def project(z_corrupt, z_clean, w_out):
    return call(
        project_kernel,
        "project",
        (z_corrupt, z_clean, w_out),
        [((HEADS_LOCAL, 2 * OWN, D), F32), ((2 * OWN, D), F32)],
        [
            VMEM((2, 16, 1024), BF16),
            VMEM((1024, D), BF16),
            pltpu.SemaphoreType.DMA((2,)),
            pltpu.SemaphoreType.DMA((HEADS_LOCAL,)),
        ],
        mib=12,
        flops=2 * 16 * 1024 * D,
        hbm=(0, 1, 2),
    )


def grad_f_kernel(cot_ref, w_ref, active_ref, out_ref, rows, acc):
    rows[...] = cot_ref[...].reshape(TOKENS * STEPS, D)
    for n in range(w_ref.shape[0] // acc.shape[0] // SIDE):
        base = n * acc.shape[0] * SIDE
        out = nt(rows[...], w_ref[base : base + acc.shape[0] * SIDE, :])
        for j in range(acc.shape[0]):
            acc[j] = out[:, j * SIDE : (j + 1) * SIDE]
            cols = slice(base + j * SIDE, base + (j + 1) * SIDE)
            act = active_ref[:, cols].astype(F32)
            for k in range(STEPS):
                out_ref[k, :, cols] = act * acc[j, pl.ds(k, TOKENS, stride=STEPS), :]


def grad_f(cot, w_dec, active):
    return call(
        grad_f_kernel,
        "grad_f",
        (cot, w_dec, active),
        [((STEPS, TOKENS, LAT_LOCAL), F32)],
        [VMEM((TOKENS * STEPS, D), BF16), VMEM((2, TOKENS * STEPS, SIDE), F32)],
        mib=8,
        flops=2 * 512 * 1024 * D,
    )[0]


def norm_kernel(a_ref, b_ref, c_ref, d_ref, rc_ref, rn_ref, gain_ref, attn_ref, msg_ref):
    attn = (a_ref[...] + b_ref[...]) + (c_ref[...] + d_ref[...])
    attn_ref[...] = attn
    first = lax.axis_index("lat") * OWN
    row = lax.broadcasted_iota(jnp.int32, (16, TOKENS), 0)
    token = lax.broadcasted_iota(jnp.int32, (16, TOKENS), 1)
    pick = ((row < 2 * OWN) & (token == first + row % OWN)).astype(F32).astype(BF16)
    corrupt = nn(pick, rc_ref[...])[: 2 * OWN]
    clean = nn(pick, rn_ref[...])[: 2 * OWN]
    upper = lax.broadcasted_iota(jnp.int32, (2 * OWN, D), 0) >= OWN
    resid = jnp.where(upper, corrupt + (clean - corrupt), corrupt)
    other = pltpu.roll(attn, OWN, 0)
    a_0 = jnp.where(upper, other, attn)
    delta = jnp.where(upper, attn, other) - a_0
    lane = lax.broadcasted_iota(jnp.int32, (2 * OWN, SIDE), 1)
    side = jnp.zeros((2 * OWN, SIDE), F32)
    invs = []
    for k in range(STEPS):
        a_k = a_0 + ALPHAS[k] * delta
        inv = lax.rsqrt(jnp.sum(a_k * a_k, axis=1, keepdims=True) * (1.0 / D) + EPSILON)
        invs.append(inv)
        side = jnp.where(lane == k, inv, side)
    low = lax.broadcasted_iota(jnp.int32, (2 * OWN, 1), 0) < OWN
    own_inv = jnp.where(low, invs[0], invs[3])
    sae_in = resid + attn * own_inv * gain_ref[...]
    msg_ref[:, :D] = sae_in
    msg_ref[:, D:] = side


def norm(parts, resid_corrupt, resid_clean, gain):
    return call(
        norm_kernel,
        "norm",
        (*parts, resid_corrupt, resid_clean, gain),
        [((2 * OWN, D), F32), ((2 * OWN, MSG), F32)],
    )


def line_kernel(a_ref, b_ref, c_ref, d_ref, out_ref):
    for d, ref in enumerate((a_ref, b_ref, c_ref, d_ref)):
        out_ref[d] = ref[...]


def line(parts):
    return call(line_kernel, "line", parts, [((4, 2 * OWN, MSG), F32)])[0]


def assemble(refs, core, out):
    x, z, _ = place()
    for e, ref in enumerate(refs):
        for d in range(4):
            from_x = (x + 4 - jnp.where(core == 0, d, e)) % 4
            from_z = (z + 4 - jnp.where(core == 0, e, d)) % 4
            out[from_x * 4 + from_z] = ref[d]


def flip_kernel(w_ref, out_ref):
    out_ref[...] = w_ref[...].T


def flip(w_enc):
    return call(flip_kernel, "flip", (w_enc,), [((LAT_LOCAL, D), BF16)])[0]


def resid_kernel(rc_ref, rn_ref, w_ref, out_ref):
    out_ref[0] = nn(rc_ref[...], w_ref[...])
    out_ref[1] = nn(rn_ref[...], w_ref[...])


def resid_project(resid_corrupt, resid_clean, w_enc):
    return call(
        resid_kernel,
        "resid_project",
        (resid_corrupt, resid_clean, w_enc),
        [((2, TOKENS, LAT_LOCAL), F32)],
        flops=2 * 256 * 1024 * D,
    )[0]


def own_kernel(a_ref, b_ref, c_ref, d_ref, w_ref, out_ref, side_ref, rows):
    assemble((a_ref, b_ref, c_ref, d_ref), place()[2], rows)
    side_ref[...] = rows[:, :, D:]
    out_ref[...] = nn(rows[:, :, :D].reshape(TOKENS, D).astype(BF16), w_ref[...])


def own_project(blocks, w_enc):
    return call(
        own_kernel,
        "own_project",
        (*blocks, w_enc),
        [((TOKENS, LAT_LOCAL), F32), ((PLANE, 2 * OWN, SIDE), F32)],
        [VMEM((PLANE, 2 * OWN, MSG), F32)],
        flops=2 * 128 * 1024 * D,
    )


def upper_rows(width):
    return lax.broadcasted_iota(jnp.int32, (TOKENS, width), 0) % 8 >= OWN


def swap_rows(x):
    width = x.shape[-1]
    return pltpu.roll(x.reshape(PLANE, 8, width), OWN, 1).reshape(TOKENS, width)


def by_step(own, other, core):
    up = upper_rows(own.shape[-1])
    is_0 = core == 0
    x_0 = jnp.where(is_0, own, other)
    x_1 = jnp.where(is_0, other, own)
    return jnp.where(up, swap_rows(x_1), x_0), jnp.where(up, x_1, swap_rows(x_0))


def by_core(x, core):
    width = x.shape[-1]
    pairs = x.reshape(PLANE // 2, 2, 8, width)
    even, odd = pairs[:, 0], pairs[:, 1]
    up = lax.broadcasted_iota(jnp.int32, even.shape, 1) >= OWN
    core_0 = jnp.where(up, pltpu.roll(odd, OWN, 1), even).reshape(TOKENS // 2, width)
    core_1 = jnp.where(up, odd, pltpu.roll(even, OWN, 1)).reshape(TOKENS // 2, width)
    is_0 = core == 0
    return jnp.where(is_0, core_0, core_1), jnp.where(is_0, core_1, core_0)


def lane_fold(x):
    total = x[:, :SIDE]
    for start in range(SIDE, x.shape[1], SIDE):
        total = total + x[:, start : start + SIDE]
    return total


def latents_kernel(
    a_ref, b_ref, c_ref, d_ref, side_ref, pre_ref, resid_ref, gf_ref, w_ref, flip_ref,
    raw_ref, keep_ref, send_ref,
    other, pre_s, hidden_s, inv_s,
):
    core = place()[2]
    assemble((a_ref, b_ref, c_ref, d_ref), 1 - core, other)
    pre_s[...] = nn(other[:, :, :D].reshape(TOKENS, D).astype(BF16), w_ref[...])
    side = by_step(
        side_ref[...].reshape(TOKENS, SIDE), other[:, :, D:].reshape(TOKENS, SIDE), core
    )[0]
    for k in range(STEPS):
        inv = jnp.broadcast_to(side[:, k : k + 1], (TOKENS, SIDE))
        inv_s[k] = inv
        inv_s[STEPS + k] = inv * inv * inv
    for k, j in ((0, 2 * STEPS), (STEPS - 1, 2 * STEPS + 1)):
        inv_s[j] = 1.0 / inv_s[k]
    tot = jnp.zeros((TOKENS, SIDE), F32)
    s_0 = jnp.zeros((TOKENS, SIDE), F32)
    s_1 = jnp.zeros((TOKENS, SIDE), F32)
    half = TOKENS // 2
    for start in range(0, LAT_LOCAL, SIDE):
        cols = slice(start, start + SIDE)
        pre_0, pre_3 = by_step(pre_ref[:, cols], pre_s[:, cols], core)
        gf = [gf_ref[k, :, cols] for k in range(STEPS)]
        raw = (pre_3 - pre_0) * (((gf[0] + gf[1]) + (gf[2] + gf[3])) * 0.25)
        raw_ref[:, cols] = raw
        tot = tot + jnp.abs(raw)
        q_0 = (pre_0 - resid_ref[0, :, cols]) * inv_s[2 * STEPS]
        q_d = (pre_3 - resid_ref[1, :, cols]) * inv_s[2 * STEPS + 1] - q_0
        u = [inv_s[STEPS + k] * gf[k] for k in range(STEPS)]
        sum_0 = (u[0] + u[1]) + (u[2] + u[3])
        sum_1 = ALPHAS[1] * u[1] + (ALPHAS[2] * u[2] + u[3])
        sum_2 = ALPHAS[1] ** 2 * u[1] + (ALPHAS[2] ** 2 * u[2] + u[3])
        s_0 = s_0 + (sum_0 * q_0 + sum_1 * q_d)
        s_1 = s_1 + (sum_1 * q_0 + sum_2 * q_d)
        hidden = (inv_s[0] * gf[0] + inv_s[1] * gf[1]) + (inv_s[2] * gf[2] + inv_s[3] * gf[3])
        first, second = by_core(hidden, core)
        hidden_s[:half, cols] = first.astype(BF16)
        hidden_s[half:, cols] = second.astype(BF16)
    grad = nn(hidden_s[...], flip_ref[...])
    keep_ref[:, :D] = grad[:half]
    send_ref[:, :D] = grad[half:]
    row = lax.broadcasted_iota(jnp.int32, (TOKENS, SIDE), 0)
    lane = lax.broadcasted_iota(jnp.int32, (TOKENS, SIDE), 1)
    tot = jnp.sum(tot, axis=1, keepdims=True)
    tot_row = jnp.sum(jnp.where(row == lane, tot, 0.0), axis=0, keepdims=True)
    tot_all = jnp.broadcast_to(tot_row, (half, SIDE))
    s_0 = jnp.sum(s_0, axis=1, keepdims=True)
    s_1 = jnp.sum(s_1, axis=1, keepdims=True)
    first, second = by_core(jnp.where(lane == 0, s_0, jnp.where(lane == 1, s_1, 0.0)), core)
    keep_ref[:, D : D + SIDE] = tot_all
    send_ref[:, D : D + SIDE] = tot_all
    keep_ref[:, D + SIDE :] = first
    send_ref[:, D + SIDE :] = second


def latents(others, side, pre_own, resid, gf, w_enc, flipped):
    half = TOKENS // 2
    return call(
        latents_kernel,
        "latents",
        (*others, side, pre_own, resid, gf, w_enc, flipped),
        [((TOKENS, LAT_LOCAL), F32), ((half, RED), F32), ((half, RED), F32)],
        [
            VMEM((PLANE, 2 * OWN, MSG), F32),
            VMEM((TOKENS, LAT_LOCAL), F32),
            VMEM((TOKENS, LAT_LOCAL), BF16),
            VMEM((2 * STEPS + 2, TOKENS, SIDE), F32),
        ],
        flops=4 * 128 * 1024 * D,
    )


def pair_kernel(a_ref, b_ref, p0_ref, p1_ref, p2_ref, p3_ref, packed):
    up = lax.broadcasted_iota(jnp.int32, (8, HALF), 0) >= OWN
    for g in range(PLANE // 2):
        tile = a_ref[8 * g : 8 * g + 8, :] + b_ref[8 * g : 8 * g + 8, :]
        left, right = tile[:, :HALF], tile[:, HALF:]
        packed[2 * g] = jnp.where(up, pltpu.roll(right, OWN, 0), left)
        packed[2 * g + 1] = jnp.where(up, right, pltpu.roll(left, OWN, 0))
    x, z, core = place()
    for d, ref in enumerate((p0_ref, p1_ref, p2_ref, p3_ref)):
        for b in range(4):
            to_x = jnp.where(core == 0, (x + d) % 4, b)
            to_z = jnp.where(core == 0, b, (z + d) % 4)
            ref[b] = packed[to_x * 4 + to_z]


def pair_sum(keep, received):
    return call(
        pair_kernel,
        "pair_sum",
        (keep, received),
        [((4, 8, HALF), F32)] * 4,
        [VMEM((PLANE, 8, HALF), F32)],
    )


def line_sum_kernel(a_ref, b_ref, c_ref, d_ref, p0_ref, p1_ref, p2_ref, p3_ref, total):
    total[...] = (a_ref[...] + b_ref[...]) + (c_ref[...] + d_ref[...])
    x, z, core = place()
    own = jnp.where(core == 0, z, x)
    for e, ref in enumerate((p0_ref, p1_ref, p2_ref, p3_ref)):
        ref[...] = total[(own + e) % 4]


def line_sum(parts):
    return call(
        line_sum_kernel, "line_sum", parts, [((8, HALF), F32)] * 4, [VMEM((4, 8, HALF), F32)]
    )


def plane_kernel(a_ref, b_ref, c_ref, d_ref, out_ref):
    out_ref[...] = (a_ref[...] + b_ref[...]) + (c_ref[...] + d_ref[...])


def plane_sum(parts):
    return call(plane_kernel, "plane_sum", parts, [((8, HALF), F32)])[0]


def result_kernel(
    a_ref, b_ref, c_ref, d_ref, attn_ref, heads_ref, gain_ref, raw_ref, latent_ref, head_ref
):
    total = (a_ref[...] + b_ref[...]) + (c_ref[...] + d_ref[...])
    rest = D - HALF
    g_left, g_right = total[:OWN], total[OWN:, :rest]
    tot_row = total[OWN : OWN + 1, rest : rest + SIDE]
    sums = total[OWN:, rest + SIDE :]
    s_0 = sums[:, 0:1] * (1.0 / D)
    s_1 = sums[:, 1:2] * (1.0 / D)
    head = jnp.zeros((OWN, HEADS_LOCAL), F32)
    lane = lax.broadcasted_iota(jnp.int32, (OWN, HEADS_LOCAL), 1)
    for part, cols in ((g_left, slice(0, HALF)), (g_right, slice(HALF, D))):
        a_0 = attn_ref[:OWN, cols]
        vec = gain_ref[:, cols] * part - (s_0 * a_0 + s_1 * (attn_ref[OWN:, cols] - a_0))
        for h in range(HEADS_LOCAL):
            v = heads_ref[h, OWN:, cols] - heads_ref[h, :OWN, cols]
            dots = jnp.sum(vec * v, axis=1, keepdims=True)
            head = head + jnp.where(lane == h, dots, 0.0)
    head_ref[...] = head * (1.0 / (HEAD_DIM * STEPS))
    row = lax.broadcasted_iota(jnp.int32, (TOKENS, SIDE), 0)
    col = lax.broadcasted_iota(jnp.int32, (TOKENS, SIDE), 1)
    tot = jnp.sum(jnp.where(row == col, tot_row, 0.0), axis=1, keepdims=True)
    latent_ref[...] = raw_ref[...] * (1.0 / (tot * (1.0 / LAT) + EPSILON))


def result(parts, attn, heads, gain, raw):
    return call(
        result_kernel,
        "result",
        (*parts, attn, heads, gain, raw),
        [((TOKENS, LAT_LOCAL), F32), ((OWN, HEADS_LOCAL), F32)],
        final=True,
    )


def over_tp(x):
    others = [lax.ppermute(x, "tp", [(i, (i + d) % 4) for i in range(4)]) for d in (1, 3, 2)]
    return [x] + others


def send(x, stage, d):
    return lax.ppermute(x, "lat", shift(stage, d))


def swap(x):
    return lax.ppermute(x, "lat", CORE_SWAP)


def body(
    z_clean, z_corrupt, resid_clean, resid_corrupt, w_out, post_gain, w_enc, w_dec, cot, active
):
    heads, part = project(z_corrupt, z_clean, w_out)
    part, post_gain, resid_clean, resid_corrupt, w_enc, w_dec, cot, active = lax.optimization_barrier(
        (part, post_gain, resid_clean, resid_corrupt, w_enc, w_dec, cot, active)
    )
    gain = post_gain.reshape(1, D)
    resid = resid_project(resid_corrupt, resid_clean, w_enc)
    *parts, resid = lax.optimization_barrier((*over_tp(part), resid))
    attn, msg = norm(parts, resid_corrupt, resid_clean, gain)
    gf = grad_f(cot, w_dec, active)
    *parts, gf = lax.optimization_barrier((msg, *[send(msg, 0, d) for d in (1, 2, 3)], gf))
    block = line(parts)
    flipped = flip(w_enc)
    blocks = [block] + [send(block, 1, e) for e in (1, 2, 3)]
    blocks[2], flipped = lax.optimization_barrier((blocks[2], flipped))
    others = [swap(b) for b in blocks]
    pre_own, side = own_project(blocks, w_enc)
    raw, keep, give = latents(others, side, pre_own, resid, gf, w_enc, flipped)
    parts = pair_sum(keep, swap(give))
    parts = line_sum([parts[0]] + [send(parts[d], 0, d) for d in (1, 2, 3)])
    total = plane_sum([parts[0]] + [send(parts[e], 1, e) for e in (1, 2, 3)])
    return tuple(result(over_tp(total), attn, heads, gain, raw))


def solution(mesh):
    placed = (
        P(None, "tp"),
        P(None, "tp"),
        P(),
        P(),
        P("tp", None),
        P(),
        P(None, ("lat", "tp")),
        P(("lat", "tp"), None),
        P(),
        P(None, ("lat", "tp")),
    )
    return jax.shard_map(
        body,
        mesh=mesh,
        in_specs=placed,
        out_specs=(P(None, ("lat", "tp")), P("lat", "tp")),
        check_vma=False,
    )
```

```python
import jax
import jax.numpy as jnp
from jax import lax
from jax.experimental import pallas as pl
from jax.experimental.pallas import tpu as pltpu
from jax.sharding import PartitionSpec as P

D = 3584
TOKENS = 128
STEPS = 4
HEAD_DIM = 256
HEADS_LOCAL = 4
LAT = 131072
LAT_LOCAL = 1024
EPSILON = 1e-06
OWN = 4
PLANE = 16
SIDE = 128
MSG = D + SIDE
RED = D + 2 * SIDE
HALF = RED // 2
ALPHAS = tuple(k / 3.0 for k in range(STEPS))
F32 = jnp.float32
BF16 = jnp.bfloat16
VMEM = pltpu.VMEM
MIB = 1024 * 1024


def lat_index(x, z, core):
    return ((x % 4) * 4 + z % 4) * 2 + core


def shift(stage, d):
    pairs = []
    for x in range(4):
        for z in range(4):
            for core in range(2):
                along_x = (stage == 0) == (core == 0)
                to = (x + d, z) if along_x else (x, z + d)
                pairs.append((lat_index(x, z, core), lat_index(*to, core)))
    return pairs


CORE_SWAP = [(i, i ^ 1) for i in range(32)]


def place():
    index = lax.axis_index("lat")
    return index // 8, (index // 2) % 4, index % 2


def call(kernel, name, operands, outs, scratch=(), mib=8, flops=10**6, hbm=(), final=False):
    spaces = [pltpu.HBM if i in hbm else VMEM for i in range(len(operands))]
    nbytes = sum(x.size * x.dtype.itemsize for x in operands)
    return pl.pallas_call(
        kernel,
        in_specs=[pl.BlockSpec(memory_space=s) for s in spaces],
        out_specs=[pl.BlockSpec(memory_space=VMEM)] * len(outs),
        out_shape=[(jax.ShapeDtypeStruct if final else VMEM)(shape, dtype) for shape, dtype in outs],
        scratch_shapes=list(scratch),
        compiler_params=pltpu.CompilerParams(vmem_limit_bytes=mib * MIB),
        cost_estimate=pl.CostEstimate(flops=flops, bytes_accessed=nbytes, transcendentals=0),
        name=name,
    )(*[pltpu.with_memory_space_constraint(x, s) for x, s in zip(operands, spaces)])


def nt(a, b):
    return lax.dot_general(a, b, (((1,), (1,)), ((), ())), preferred_element_type=F32)


def nn(a, b):
    return lax.dot_general(a, b, (((1,), (0,)), ((), ())), preferred_element_type=F32)


def project_kernel(zc_ref, zn_ref, w_ref, heads_ref, part_ref, z_s, w_s, z_sems, sems):
    index = lax.axis_index("lat")
    block = pl.ds(pl.multiple_of((index // 4) * 16, 16), 16)
    z_copies = [
        pltpu.make_async_copy(ref.at[block, :], z_s.at[i], z_sems.at[i])
        for i, ref in enumerate((zc_ref, zn_ref))
    ]
    for copy in z_copies:
        copy.start()
    copies = []
    for h in range(HEADS_LOCAL):
        rows = pl.ds(h * HEAD_DIM, HEAD_DIM)
        copies.append(pltpu.make_async_copy(w_ref.at[rows, :], w_s.at[rows, :], sems.at[h]))
        copies[-1].start()
    first = (index % 4) * OWN
    row = lax.broadcasted_iota(jnp.int32, (16, 16), 0)
    token = lax.broadcasted_iota(jnp.int32, (16, 16), 1)
    pick_c = ((row < OWN) & (token == first + row)).astype(F32).astype(BF16)
    pick_n = ((row >= OWN) & (row < 2 * OWN) & (token == first + row - OWN)).astype(F32).astype(BF16)
    for copy in z_copies:
        copy.wait()
    z = (nn(pick_c, z_s[0]) + nn(pick_n, z_s[1])).astype(BF16)
    for h in range(HEADS_LOCAL):
        copies[h].wait()
        cols = slice(h * HEAD_DIM, (h + 1) * HEAD_DIM)
        out = nn(z[:, cols], w_s[cols, :])[: 2 * OWN]
        heads_ref[h] = out
        if h == 0:
            part_ref[...] = out
        else:
            part_ref[...] += out


def project(z_corrupt, z_clean, w_out):
    return call(
        project_kernel,
        "project",
        (z_corrupt, z_clean, w_out),
        [((HEADS_LOCAL, 2 * OWN, D), F32), ((2 * OWN, D), F32)],
        [
            VMEM((2, 16, 1024), BF16),
            VMEM((1024, D), BF16),
            pltpu.SemaphoreType.DMA((2,)),
            pltpu.SemaphoreType.DMA((HEADS_LOCAL,)),
        ],
        mib=12,
        flops=2 * 16 * 1024 * D,
        hbm=(0, 1, 2),
    )


def grad_f_kernel(cot_ref, w_ref, active_ref, out_ref, rows, acc):
    rows[...] = cot_ref[...].reshape(TOKENS * STEPS, D)
    for n in range(w_ref.shape[0] // acc.shape[0] // SIDE):
        base = n * acc.shape[0] * SIDE
        out = nt(rows[...], w_ref[base : base + acc.shape[0] * SIDE, :])
        for j in range(acc.shape[0]):
            acc[j] = out[:, j * SIDE : (j + 1) * SIDE]
            cols = slice(base + j * SIDE, base + (j + 1) * SIDE)
            act = active_ref[:, cols].astype(F32)
            for k in range(STEPS):
                out_ref[k, :, cols] = act * acc[j, pl.ds(k, TOKENS, stride=STEPS), :]


def grad_f(cot, w_dec, active):
    return call(
        grad_f_kernel,
        "grad_f",
        (cot, w_dec, active),
        [((STEPS, TOKENS, LAT_LOCAL), F32)],
        [VMEM((TOKENS * STEPS, D), BF16), VMEM((2, TOKENS * STEPS, SIDE), F32)],
        mib=8,
        flops=2 * 512 * 1024 * D,
    )[0]


def norm_kernel(a_ref, b_ref, c_ref, d_ref, rc_ref, rn_ref, gain_ref, attn_ref, msg_ref):
    attn = (a_ref[...] + b_ref[...]) + (c_ref[...] + d_ref[...])
    attn_ref[...] = attn
    first = lax.axis_index("lat") * OWN
    row = lax.broadcasted_iota(jnp.int32, (16, TOKENS), 0)
    token = lax.broadcasted_iota(jnp.int32, (16, TOKENS), 1)
    pick = ((row < 2 * OWN) & (token == first + row % OWN)).astype(F32).astype(BF16)
    corrupt = nn(pick, rc_ref[...])[: 2 * OWN]
    clean = nn(pick, rn_ref[...])[: 2 * OWN]
    upper = lax.broadcasted_iota(jnp.int32, (2 * OWN, D), 0) >= OWN
    resid = jnp.where(upper, corrupt + (clean - corrupt), corrupt)
    other = pltpu.roll(attn, OWN, 0)
    a_0 = jnp.where(upper, other, attn)
    delta = jnp.where(upper, attn, other) - a_0
    lane = lax.broadcasted_iota(jnp.int32, (2 * OWN, SIDE), 1)
    side = jnp.zeros((2 * OWN, SIDE), F32)
    invs = []
    for k in range(STEPS):
        a_k = a_0 + ALPHAS[k] * delta
        inv = lax.rsqrt(jnp.sum(a_k * a_k, axis=1, keepdims=True) * (1.0 / D) + EPSILON)
        invs.append(inv)
        side = jnp.where(lane == k, inv, side)
    low = lax.broadcasted_iota(jnp.int32, (2 * OWN, 1), 0) < OWN
    own_inv = jnp.where(low, invs[0], invs[3])
    sae_in = resid + attn * own_inv * gain_ref[...]
    msg_ref[:, :D] = sae_in
    msg_ref[:, D:] = side


def norm(parts, resid_corrupt, resid_clean, gain):
    return call(
        norm_kernel,
        "norm",
        (*parts, resid_corrupt, resid_clean, gain),
        [((2 * OWN, D), F32), ((2 * OWN, MSG), F32)],
    )


def line_kernel(a_ref, b_ref, c_ref, d_ref, out_ref):
    for d, ref in zip((0, *(1,2,3)), (a_ref, b_ref, c_ref, d_ref)):
        out_ref[d] = ref[...]


def line(parts):
    return call(line_kernel, "line", parts, [((4, 2 * OWN, MSG), F32)])[0]


def assemble(refs, core, out):
    x, z, _ = place()
    for e, ref in enumerate(refs):
        for d in range(4):
            from_x = (x + 4 - jnp.where(core == 0, d, e)) % 4
            from_z = (z + 4 - jnp.where(core == 0, e, d)) % 4
            out[from_x * 4 + from_z] = ref[d]


def flip_kernel(w_ref, out_ref):
    out_ref[...] = w_ref[...].T


def flip(w_enc):
    return call(flip_kernel, "flip", (w_enc,), [((LAT_LOCAL, D), BF16)])[0]


def resid_kernel(rc_ref, rn_ref, w_ref, out_ref):
    out_ref[0] = nn(rc_ref[...], w_ref[...])
    out_ref[1] = nn(rn_ref[...], w_ref[...])


def resid_project(resid_corrupt, resid_clean, w_enc):
    return call(
        resid_kernel,
        "resid_project",
        (resid_corrupt, resid_clean, w_enc),
        [((2, TOKENS, LAT_LOCAL), F32)],
        flops=2 * 256 * 1024 * D,
    )[0]


def own_kernel(a_ref, b_ref, c_ref, d_ref, w_ref, out_ref, side_ref, rows):
    assemble((a_ref, b_ref, c_ref, d_ref), place()[2], rows)
    side_ref[...] = rows[:, :, D:]
    out_ref[...] = nn(rows[:, :, :D].reshape(TOKENS, D).astype(BF16), w_ref[...])


def own_project(blocks, w_enc):
    return call(
        own_kernel,
        "own_project",
        (*blocks, w_enc),
        [((TOKENS, LAT_LOCAL), F32), ((PLANE, 2 * OWN, SIDE), F32)],
        [VMEM((PLANE, 2 * OWN, MSG), F32)],
        flops=2 * 128 * 1024 * D,
    )


def upper_rows(width):
    return lax.broadcasted_iota(jnp.int32, (TOKENS, width), 0) % 8 >= OWN


def swap_rows(x):
    width = x.shape[-1]
    return pltpu.roll(x.reshape(PLANE, 8, width), OWN, 1).reshape(TOKENS, width)


def by_step(own, other, core):
    up = upper_rows(own.shape[-1])
    is_0 = core == 0
    x_0 = jnp.where(is_0, own, other)
    x_1 = jnp.where(is_0, other, own)
    return jnp.where(up, swap_rows(x_1), x_0), jnp.where(up, x_1, swap_rows(x_0))


def by_core(x, core):
    width = x.shape[-1]
    pairs = x.reshape(PLANE // 2, 2, 8, width)
    even, odd = pairs[:, 0], pairs[:, 1]
    up = lax.broadcasted_iota(jnp.int32, even.shape, 1) >= OWN
    core_0 = jnp.where(up, pltpu.roll(odd, OWN, 1), even).reshape(TOKENS // 2, width)
    core_1 = jnp.where(up, odd, pltpu.roll(even, OWN, 1)).reshape(TOKENS // 2, width)
    is_0 = core == 0
    return jnp.where(is_0, core_0, core_1), jnp.where(is_0, core_1, core_0)


def lane_fold(x):
    total = x[:, :SIDE]
    for start in range(SIDE, x.shape[1], SIDE):
        total = total + x[:, start : start + SIDE]
    return total


def latents_kernel(
    a_ref, b_ref, c_ref, d_ref, side_ref, pre_ref, resid_ref, gf_ref, w_ref, flip_ref,
    raw_ref, keep_ref, send_ref,
    other, pre_s, hidden_s, inv_s,
):
    core = place()[2]
    assemble((a_ref, b_ref, c_ref, d_ref), 1 - core, other)
    pre_s[...] = nn(other[:, :, :D].reshape(TOKENS, D).astype(BF16), w_ref[...])
    side = by_step(
        side_ref[...].reshape(TOKENS, SIDE), other[:, :, D:].reshape(TOKENS, SIDE), core
    )[0]
    for k in range(STEPS):
        inv = jnp.broadcast_to(side[:, k : k + 1], (TOKENS, SIDE))
        inv_s[k] = inv
        inv_s[STEPS + k] = inv * inv * inv
    for k, j in ((0, 2 * STEPS), (STEPS - 1, 2 * STEPS + 1)):
        inv_s[j] = 1.0 / inv_s[k]
    tot = jnp.zeros((TOKENS, SIDE), F32)
    s_0 = jnp.zeros((TOKENS, SIDE), F32)
    s_1 = jnp.zeros((TOKENS, SIDE), F32)
    half = TOKENS // 2
    for start in range(0, LAT_LOCAL, SIDE):
        cols = slice(start, start + SIDE)
        pre_0, pre_3 = by_step(pre_ref[:, cols], pre_s[:, cols], core)
        gf = [gf_ref[k, :, cols] for k in range(STEPS)]
        raw = (pre_3 - pre_0) * (((gf[0] + gf[1]) + (gf[2] + gf[3])) * 0.25)
        raw_ref[:, cols] = raw
        tot = tot + jnp.abs(raw)
        q_0 = (pre_0 - resid_ref[0, :, cols]) * inv_s[2 * STEPS]
        q_d = (pre_3 - resid_ref[1, :, cols]) * inv_s[2 * STEPS + 1] - q_0
        u = [inv_s[STEPS + k] * gf[k] for k in range(STEPS)]
        sum_0 = (u[0] + u[1]) + (u[2] + u[3])
        sum_1 = ALPHAS[1] * u[1] + (ALPHAS[2] * u[2] + u[3])
        sum_2 = ALPHAS[1] ** 2 * u[1] + (ALPHAS[2] ** 2 * u[2] + u[3])
        s_0 = s_0 + (sum_0 * q_0 + sum_1 * q_d)
        s_1 = s_1 + (sum_1 * q_0 + sum_2 * q_d)
        hidden = (inv_s[0] * gf[0] + inv_s[1] * gf[1]) + (inv_s[2] * gf[2] + inv_s[3] * gf[3])
        first, second = by_core(hidden, core)
        hidden_s[:half, cols] = first.astype(BF16)
        hidden_s[half:, cols] = second.astype(BF16)
    grad = nn(hidden_s[...], flip_ref[...])
    keep_ref[:, :D] = grad[:half]
    send_ref[:, :D] = grad[half:]
    row = lax.broadcasted_iota(jnp.int32, (TOKENS, SIDE), 0)
    lane = lax.broadcasted_iota(jnp.int32, (TOKENS, SIDE), 1)
    tot = jnp.sum(tot, axis=1, keepdims=True)
    tot_row = jnp.sum(jnp.where(row == lane, tot, 0.0), axis=0, keepdims=True)
    tot_all = jnp.broadcast_to(tot_row, (half, SIDE))
    s_0 = jnp.sum(s_0, axis=1, keepdims=True)
    s_1 = jnp.sum(s_1, axis=1, keepdims=True)
    first, second = by_core(jnp.where(lane == 0, s_0, jnp.where(lane == 1, s_1, 0.0)), core)
    keep_ref[:, D : D + SIDE] = tot_all
    send_ref[:, D : D + SIDE] = tot_all
    keep_ref[:, D + SIDE :] = first
    send_ref[:, D + SIDE :] = second


def latents(others, side, pre_own, resid, gf, w_enc, flipped):
    half = TOKENS // 2
    return call(
        latents_kernel,
        "latents",
        (*others, side, pre_own, resid, gf, w_enc, flipped),
        [((TOKENS, LAT_LOCAL), F32), ((half, RED), F32), ((half, RED), F32)],
        [
            VMEM((PLANE, 2 * OWN, MSG), F32),
            VMEM((TOKENS, LAT_LOCAL), F32),
            VMEM((TOKENS, LAT_LOCAL), BF16),
            VMEM((2 * STEPS + 2, TOKENS, SIDE), F32),
        ],
        flops=4 * 128 * 1024 * D,
    )


def pair_kernel(a_ref, b_ref, p0_ref, p1_ref, p2_ref, p3_ref, packed):
    up = lax.broadcasted_iota(jnp.int32, (8, HALF), 0) >= OWN
    for g in range(PLANE // 2):
        tile = a_ref[8 * g : 8 * g + 8, :] + b_ref[8 * g : 8 * g + 8, :]
        left, right = tile[:, :HALF], tile[:, HALF:]
        packed[2 * g] = jnp.where(up, pltpu.roll(right, OWN, 0), left)
        packed[2 * g + 1] = jnp.where(up, right, pltpu.roll(left, OWN, 0))
    x, z, core = place()
    for d, ref in enumerate((p0_ref, p1_ref, p2_ref, p3_ref)):
        for b in range(4):
            to_x = jnp.where(core == 0, (x + d) % 4, b)
            to_z = jnp.where(core == 0, b, (z + d) % 4)
            ref[b] = packed[to_x * 4 + to_z]


def pair_sum(keep, received):
    return call(
        pair_kernel,
        "pair_sum",
        (keep, received),
        [((4, 8, HALF), F32)] * 4,
        [VMEM((PLANE, 8, HALF), F32)],
    )


def line_sum_kernel(a_ref, b_ref, c_ref, d_ref, p0_ref, p1_ref, p2_ref, p3_ref, total):
    total[...] = (a_ref[...] + b_ref[...]) + (c_ref[...] + d_ref[...])
    x, z, core = place()
    own = jnp.where(core == 0, z, x)
    for e, ref in enumerate((p0_ref, p1_ref, p2_ref, p3_ref)):
        ref[...] = total[(own + e) % 4]


def line_sum(parts):
    return call(
        line_sum_kernel, "line_sum", parts, [((8, HALF), F32)] * 4, [VMEM((4, 8, HALF), F32)]
    )


def plane_kernel(a_ref, b_ref, c_ref, d_ref, out_ref):
    out_ref[...] = (a_ref[...] + b_ref[...]) + (c_ref[...] + d_ref[...])


def plane_sum(parts):
    return call(plane_kernel, "plane_sum", parts, [((8, HALF), F32)])[0]


def result_kernel(
    a_ref, b_ref, c_ref, d_ref, attn_ref, heads_ref, gain_ref, raw_ref, latent_ref, head_ref
):
    total = (a_ref[...] + b_ref[...]) + (c_ref[...] + d_ref[...])
    rest = D - HALF
    g_left, g_right = total[:OWN], total[OWN:, :rest]
    tot_row = total[OWN : OWN + 1, rest : rest + SIDE]
    sums = total[OWN:, rest + SIDE :]
    s_0 = sums[:, 0:1] * (1.0 / D)
    s_1 = sums[:, 1:2] * (1.0 / D)
    head = jnp.zeros((OWN, HEADS_LOCAL), F32)
    lane = lax.broadcasted_iota(jnp.int32, (OWN, HEADS_LOCAL), 1)
    for part, cols in ((g_left, slice(0, HALF)), (g_right, slice(HALF, D))):
        a_0 = attn_ref[:OWN, cols]
        vec = gain_ref[:, cols] * part - (s_0 * a_0 + s_1 * (attn_ref[OWN:, cols] - a_0))
        for h in range(HEADS_LOCAL):
            v = heads_ref[h, OWN:, cols] - heads_ref[h, :OWN, cols]
            dots = jnp.sum(vec * v, axis=1, keepdims=True)
            head = head + jnp.where(lane == h, dots, 0.0)
    head_ref[...] = head * (1.0 / (HEAD_DIM * STEPS))
    row = lax.broadcasted_iota(jnp.int32, (TOKENS, SIDE), 0)
    col = lax.broadcasted_iota(jnp.int32, (TOKENS, SIDE), 1)
    tot = jnp.sum(jnp.where(row == col, tot_row, 0.0), axis=1, keepdims=True)
    latent_ref[...] = raw_ref[...] * (1.0 / (tot * (1.0 / LAT) + EPSILON))


def result(parts, attn, heads, gain, raw):
    return call(
        result_kernel,
        "result",
        (*parts, attn, heads, gain, raw),
        [((TOKENS, LAT_LOCAL), F32), ((OWN, HEADS_LOCAL), F32)],
        final=True,
    )


def over_tp(x, order):
    others = [lax.ppermute(x, "tp", [(i, (i + d) % 4) for i in range(4)]) for d in order]
    return [x] + others


def send(x, stage, d):
    return lax.ppermute(x, "lat", shift(stage, d))


def swap(x):
    return lax.ppermute(x, "lat", CORE_SWAP)


def body(
    z_clean, z_corrupt, resid_clean, resid_corrupt, w_out, post_gain, w_enc, w_dec, cot, active
):
    heads, part = project(z_corrupt, z_clean, w_out)
    part, post_gain, resid_clean, resid_corrupt, w_enc, w_dec, cot, active = lax.optimization_barrier(
        (part, post_gain, resid_clean, resid_corrupt, w_enc, w_dec, cot, active)
    )
    gain = post_gain.reshape(1, D)
    resid = resid_project(resid_corrupt, resid_clean, w_enc)
    *parts, resid = lax.optimization_barrier((*over_tp(part, (3,1,2)), resid))
    attn, msg = norm(parts, resid_corrupt, resid_clean, gain)
    gf = grad_f(cot, w_dec, active)
    parts = [msg] + [send(msg, 0, d) for d in (1,2,3)]
    *parts, gf = lax.optimization_barrier((*parts, gf))
    block = line(parts)
    flipped = flip(w_enc)
    blocks = [block] + [send(block, 1, e) for e in (1, 2, 3)]
    blocks[2], flipped = lax.optimization_barrier((blocks[2], flipped))
    others = [swap(b) for b in blocks]
    *blocks, others[2] = lax.optimization_barrier((*blocks, others[2]))
    pre_own, side = own_project(blocks, w_enc)
    raw, keep, give = latents(others, side, pre_own, resid, gf, w_enc, flipped)
    parts = pair_sum(keep, swap(give))
    parts = line_sum([parts[0]] + [send(parts[d], 0, d) for d in (2,1,3)])
    total = plane_sum([parts[0]] + [send(parts[e], 1, e) for e in (2,1,3)])
    return tuple(result(over_tp(total, (3,1,2)), attn, heads, gain, raw))


def solution(mesh):
    placed = (
        P(None, "tp"),
        P(None, "tp"),
        P(),
        P(),
        P("tp", None),
        P(),
        P(None, ("lat", "tp")),
        P(("lat", "tp"), None),
        P(),
        P(None, ("lat", "tp")),
    )
    return jax.shard_map(
        body,
        mesh=mesh,
        in_specs=placed,
        out_specs=(P(None, ("lat", "tp")), P("lat", "tp")),
        check_vma=False,
    )
```

```python
import jax
import jax.numpy as jnp
from jax import lax
from jax.experimental import pallas as pl
from jax.experimental.pallas import tpu as pltpu
from jax.sharding import PartitionSpec as P

D = 3584
TOKENS = 128
STEPS = 4
HEAD_DIM = 256
HEADS_LOCAL = 4
LAT = 131072
LAT_LOCAL = 1024
EPSILON = 1e-06
OWN = 4
PLANE = 16
SIDE = 128
MSG = D + SIDE
RED = D + 2 * SIDE
HALF = RED // 2
ALPHAS = tuple(k / 3.0 for k in range(STEPS))
F32 = jnp.float32
BF16 = jnp.bfloat16
VMEM = pltpu.VMEM
MIB = 1024 * 1024


def lat_index(x, z, core):
    return ((x % 4) * 4 + z % 4) * 2 + core


def shift(stage, d):
    pairs = []
    for x in range(4):
        for z in range(4):
            for core in range(2):
                along_x = (stage == 0) == (core == 0)
                to = (x + d, z) if along_x else (x, z + d)
                pairs.append((lat_index(x, z, core), lat_index(*to, core)))
    return pairs


CORE_SWAP = [(i, i ^ 1) for i in range(32)]


def place():
    index = lax.axis_index("lat")
    return index // 8, (index // 2) % 4, index % 2


def call(kernel, name, operands, outs, scratch=(), mib=8, flops=10**6, hbm=(), final=False):
    spaces = [pltpu.HBM if i in hbm else VMEM for i in range(len(operands))]
    nbytes = sum(x.size * x.dtype.itemsize for x in operands)
    return pl.pallas_call(
        kernel,
        in_specs=[pl.BlockSpec(memory_space=s) for s in spaces],
        out_specs=[pl.BlockSpec(memory_space=VMEM)] * len(outs),
        out_shape=[(jax.ShapeDtypeStruct if final else VMEM)(shape, dtype) for shape, dtype in outs],
        scratch_shapes=list(scratch),
        compiler_params=pltpu.CompilerParams(vmem_limit_bytes=mib * MIB),
        cost_estimate=pl.CostEstimate(flops=flops, bytes_accessed=nbytes, transcendentals=0),
        name=name,
    )(*[pltpu.with_memory_space_constraint(x, s) for x, s in zip(operands, spaces)])


def nt(a, b):
    return lax.dot_general(a, b, (((1,), (1,)), ((), ())), preferred_element_type=F32)


def nn(a, b):
    return lax.dot_general(a, b, (((1,), (0,)), ((), ())), preferred_element_type=F32)


def project_kernel(zc_ref, zn_ref, w_ref, heads_ref, part_ref, z_s, w_s, z_sems, sems):
    index = lax.axis_index("lat")
    block = pl.ds(pl.multiple_of((index // 4) * 16, 16), 16)
    z_copies = [
        pltpu.make_async_copy(ref.at[block, :], z_s.at[i], z_sems.at[i])
        for i, ref in enumerate((zc_ref, zn_ref))
    ]
    for copy in z_copies:
        copy.start()
    copies = []
    for i in range(2):
        rows = pl.ds(i * 2 * HEAD_DIM, 2 * HEAD_DIM)
        copies.append(pltpu.make_async_copy(w_ref.at[rows, :], w_s.at[rows, :], sems.at[i]))
        copies[-1].start()
    first = (index % 4) * OWN
    row = lax.broadcasted_iota(jnp.int32, (16, 16), 0)
    token = lax.broadcasted_iota(jnp.int32, (16, 16), 1)
    pick_c = ((row < OWN) & (token == first + row)).astype(F32).astype(BF16)
    pick_n = ((row >= OWN) & (row < 2 * OWN) & (token == first + row - OWN)).astype(F32).astype(BF16)
    for copy in z_copies:
        copy.wait()
    z = (nn(pick_c, z_s[0]) + nn(pick_n, z_s[1])).astype(BF16)
    for h in range(HEADS_LOCAL):
        if h % 2 == 0:
            copies[h // 2].wait()
        cols = slice(h * HEAD_DIM, (h + 1) * HEAD_DIM)
        out = nn(z[:, cols], w_s[cols, :])[: 2 * OWN]
        heads_ref[h] = out
        if h == 0:
            part_ref[...] = out
        else:
            part_ref[...] += out


def project(z_corrupt, z_clean, w_out):
    return call(
        project_kernel,
        "project",
        (z_corrupt, z_clean, w_out),
        [((HEADS_LOCAL, 2 * OWN, D), F32), ((2 * OWN, D), F32)],
        [
            VMEM((2, 16, 1024), BF16),
            VMEM((1024, D), BF16),
            pltpu.SemaphoreType.DMA((2,)),
            pltpu.SemaphoreType.DMA((2,)),
        ],
        mib=12,
        flops=2 * 16 * 1024 * D,
        hbm=(0, 1, 2),
    )


def grad_f_kernel(cot_ref, w_ref, active_ref, out_ref, rows, acc):
    rows[...] = cot_ref[...].reshape(TOKENS * STEPS, D)
    for n in range(w_ref.shape[0] // acc.shape[0] // SIDE):
        base = n * acc.shape[0] * SIDE
        out = nt(rows[...], w_ref[base : base + acc.shape[0] * SIDE, :])
        for j in range(acc.shape[0]):
            acc[j] = out[:, j * SIDE : (j + 1) * SIDE]
            cols = slice(base + j * SIDE, base + (j + 1) * SIDE)
            act = active_ref[:, cols].astype(F32)
            for k in range(STEPS):
                out_ref[k, :, cols] = act * acc[j, pl.ds(k, TOKENS, stride=STEPS), :]


def grad_f(cot, w_dec, active):
    return call(
        grad_f_kernel,
        "grad_f",
        (cot, w_dec, active),
        [((STEPS, TOKENS, LAT_LOCAL), F32)],
        [VMEM((TOKENS * STEPS, D), BF16), VMEM((2, TOKENS * STEPS, SIDE), F32)],
        mib=8,
        flops=2 * 512 * 1024 * D,
    )[0]


def norm_kernel(a_ref, b_ref, c_ref, d_ref, rc_ref, rn_ref, gain_ref, attn_ref, msg_ref):
    attn = (a_ref[...] + b_ref[...]) + (c_ref[...] + d_ref[...])
    attn_ref[...] = attn
    first = lax.axis_index("lat") * OWN
    row = lax.broadcasted_iota(jnp.int32, (16, TOKENS), 0)
    token = lax.broadcasted_iota(jnp.int32, (16, TOKENS), 1)
    pick = ((row < 2 * OWN) & (token == first + row % OWN)).astype(F32).astype(BF16)
    corrupt = nn(pick, rc_ref[...])[: 2 * OWN]
    clean = nn(pick, rn_ref[...])[: 2 * OWN]
    upper = lax.broadcasted_iota(jnp.int32, (2 * OWN, D), 0) >= OWN
    resid = jnp.where(upper, corrupt + (clean - corrupt), corrupt)
    other = pltpu.roll(attn, OWN, 0)
    a_0 = jnp.where(upper, other, attn)
    delta = jnp.where(upper, attn, other) - a_0
    lane = lax.broadcasted_iota(jnp.int32, (2 * OWN, SIDE), 1)
    side = jnp.zeros((2 * OWN, SIDE), F32)
    invs = []
    for k in range(STEPS):
        a_k = a_0 + ALPHAS[k] * delta
        inv = lax.rsqrt(jnp.sum(a_k * a_k, axis=1, keepdims=True) * (1.0 / D) + EPSILON)
        invs.append(inv)
        side = jnp.where(lane == k, inv, side)
    low = lax.broadcasted_iota(jnp.int32, (2 * OWN, 1), 0) < OWN
    own_inv = jnp.where(low, invs[0], invs[3])
    sae_in = resid + attn * own_inv * gain_ref[...]
    msg_ref[:, :D] = sae_in
    msg_ref[:, D:] = side


def norm(parts, resid_corrupt, resid_clean, gain):
    return call(
        norm_kernel,
        "norm",
        (*parts, resid_corrupt, resid_clean, gain),
        [((2 * OWN, D), F32), ((2 * OWN, MSG), F32)],
    )


def line_kernel(a_ref, b_ref, c_ref, d_ref, out_ref):
    for d, ref in zip((0, *(3,2,1)), (a_ref, b_ref, c_ref, d_ref)):
        out_ref[d] = ref[...]


def line(parts):
    return call(line_kernel, "line", parts, [((4, 2 * OWN, MSG), F32)])[0]


def assemble(refs, core, out):
    x, z, _ = place()
    for e, ref in enumerate(refs):
        for d in range(4):
            from_x = (x + 4 - jnp.where(core == 0, d, e)) % 4
            from_z = (z + 4 - jnp.where(core == 0, e, d)) % 4
            out[from_x * 4 + from_z] = ref[d]


def flip_kernel(w_ref, out_ref):
    out_ref[...] = w_ref[...].T


def flip(w_enc):
    return call(flip_kernel, "flip", (w_enc,), [((LAT_LOCAL, D), BF16)])[0]


def resid_kernel(rc_ref, rn_ref, w_ref, out_ref):
    out_ref[0] = nn(rc_ref[...], w_ref[...])
    out_ref[1] = nn(rn_ref[...], w_ref[...])


def resid_project(resid_corrupt, resid_clean, w_enc):
    return call(
        resid_kernel,
        "resid_project",
        (resid_corrupt, resid_clean, w_enc),
        [((2, TOKENS, LAT_LOCAL), F32)],
        flops=2 * 256 * 1024 * D,
    )[0]


def own_kernel(a_ref, b_ref, c_ref, d_ref, w_ref, out_ref, side_ref, rows):
    assemble((a_ref, b_ref, c_ref, d_ref), place()[2], rows)
    side_ref[...] = rows[:, :, D:]
    out_ref[...] = nn(rows[:, :, :D].reshape(TOKENS, D).astype(BF16), w_ref[...])


def own_project(blocks, w_enc):
    return call(
        own_kernel,
        "own_project",
        (*blocks, w_enc),
        [((TOKENS, LAT_LOCAL), F32), ((PLANE, 2 * OWN, SIDE), F32)],
        [VMEM((PLANE, 2 * OWN, MSG), F32)],
        flops=2 * 128 * 1024 * D,
    )


def upper_rows(width):
    return lax.broadcasted_iota(jnp.int32, (TOKENS, width), 0) % 8 >= OWN


def swap_rows(x):
    width = x.shape[-1]
    return pltpu.roll(x.reshape(PLANE, 8, width), OWN, 1).reshape(TOKENS, width)


def by_step(own, other, core):
    up = upper_rows(own.shape[-1])
    is_0 = core == 0
    x_0 = jnp.where(is_0, own, other)
    x_1 = jnp.where(is_0, other, own)
    return jnp.where(up, swap_rows(x_1), x_0), jnp.where(up, x_1, swap_rows(x_0))


def by_core(x, core):
    width = x.shape[-1]
    pairs = x.reshape(PLANE // 2, 2, 8, width)
    even, odd = pairs[:, 0], pairs[:, 1]
    up = lax.broadcasted_iota(jnp.int32, even.shape, 1) >= OWN
    core_0 = jnp.where(up, pltpu.roll(odd, OWN, 1), even).reshape(TOKENS // 2, width)
    core_1 = jnp.where(up, odd, pltpu.roll(even, OWN, 1)).reshape(TOKENS // 2, width)
    is_0 = core == 0
    return jnp.where(is_0, core_0, core_1), jnp.where(is_0, core_1, core_0)


def lane_fold(x):
    total = x[:, :SIDE]
    for start in range(SIDE, x.shape[1], SIDE):
        total = total + x[:, start : start + SIDE]
    return total


def latents_kernel(
    a_ref, b_ref, c_ref, d_ref, side_ref, pre_ref, resid_ref, gf_ref, w_ref, flip_ref,
    raw_ref, keep_ref, send_ref,
    other, pre_s, hidden_s, inv_s,
):
    core = place()[2]
    assemble((a_ref, b_ref, c_ref, d_ref), 1 - core, other)
    pre_s[...] = nn(other[:, :, :D].reshape(TOKENS, D).astype(BF16), w_ref[...])
    side = by_step(
        side_ref[...].reshape(TOKENS, SIDE), other[:, :, D:].reshape(TOKENS, SIDE), core
    )[0]
    for k in range(STEPS):
        inv = jnp.broadcast_to(side[:, k : k + 1], (TOKENS, SIDE))
        inv_s[k] = inv
        inv_s[STEPS + k] = inv * inv * inv
    for k, j in ((0, 2 * STEPS), (STEPS - 1, 2 * STEPS + 1)):
        inv_s[j] = 1.0 / inv_s[k]
    tot = jnp.zeros((TOKENS, SIDE), F32)
    s_0 = jnp.zeros((TOKENS, SIDE), F32)
    s_1 = jnp.zeros((TOKENS, SIDE), F32)
    half = TOKENS // 2
    for start in range(0, LAT_LOCAL, SIDE):
        cols = slice(start, start + SIDE)
        pre_0, pre_3 = by_step(pre_ref[:, cols], pre_s[:, cols], core)
        gf = [gf_ref[k, :, cols] for k in range(STEPS)]
        raw = (pre_3 - pre_0) * (((gf[0] + gf[1]) + (gf[2] + gf[3])) * 0.25)
        raw_ref[:, cols] = raw
        tot = tot + jnp.abs(raw)
        q_0 = (pre_0 - resid_ref[0, :, cols]) * inv_s[2 * STEPS]
        q_d = (pre_3 - resid_ref[1, :, cols]) * inv_s[2 * STEPS + 1] - q_0
        u = [inv_s[STEPS + k] * gf[k] for k in range(STEPS)]
        sum_0 = (u[0] + u[1]) + (u[2] + u[3])
        sum_1 = ALPHAS[1] * u[1] + (ALPHAS[2] * u[2] + u[3])
        sum_2 = ALPHAS[1] ** 2 * u[1] + (ALPHAS[2] ** 2 * u[2] + u[3])
        s_0 = s_0 + (sum_0 * q_0 + sum_1 * q_d)
        s_1 = s_1 + (sum_1 * q_0 + sum_2 * q_d)
        hidden = (inv_s[0] * gf[0] + inv_s[1] * gf[1]) + (inv_s[2] * gf[2] + inv_s[3] * gf[3])
        first, second = by_core(hidden, core)
        hidden_s[:half, cols] = first.astype(BF16)
        hidden_s[half:, cols] = second.astype(BF16)
    grad = nn(hidden_s[...], flip_ref[...])
    keep_ref[:, :D] = grad[:half]
    send_ref[:, :D] = grad[half:]
    row = lax.broadcasted_iota(jnp.int32, (TOKENS, SIDE), 0)
    lane = lax.broadcasted_iota(jnp.int32, (TOKENS, SIDE), 1)
    tot = jnp.sum(tot, axis=1, keepdims=True)
    tot_row = jnp.sum(jnp.where(row == lane, tot, 0.0), axis=0, keepdims=True)
    tot_all = jnp.broadcast_to(tot_row, (half, SIDE))
    s_0 = jnp.sum(s_0, axis=1, keepdims=True)
    s_1 = jnp.sum(s_1, axis=1, keepdims=True)
    first, second = by_core(jnp.where(lane == 0, s_0, jnp.where(lane == 1, s_1, 0.0)), core)
    keep_ref[:, D : D + SIDE] = tot_all
    send_ref[:, D : D + SIDE] = tot_all
    keep_ref[:, D + SIDE :] = first
    send_ref[:, D + SIDE :] = second


def latents(others, side, pre_own, resid, gf, w_enc, flipped):
    half = TOKENS // 2
    return call(
        latents_kernel,
        "latents",
        (*others, side, pre_own, resid, gf, w_enc, flipped),
        [((TOKENS, LAT_LOCAL), F32), ((half, RED), F32), ((half, RED), F32)],
        [
            VMEM((PLANE, 2 * OWN, MSG), F32),
            VMEM((TOKENS, LAT_LOCAL), F32),
            VMEM((TOKENS, LAT_LOCAL), BF16),
            VMEM((2 * STEPS + 2, TOKENS, SIDE), F32),
        ],
        flops=4 * 128 * 1024 * D,
    )


def pair_kernel(a_ref, b_ref, p0_ref, p1_ref, p2_ref, p3_ref, packed):
    up = lax.broadcasted_iota(jnp.int32, (8, HALF), 0) >= OWN
    for g in range(PLANE // 2):
        tile = a_ref[8 * g : 8 * g + 8, :] + b_ref[8 * g : 8 * g + 8, :]
        left, right = tile[:, :HALF], tile[:, HALF:]
        packed[2 * g] = jnp.where(up, pltpu.roll(right, OWN, 0), left)
        packed[2 * g + 1] = jnp.where(up, right, pltpu.roll(left, OWN, 0))
    x, z, core = place()
    for d, ref in enumerate((p0_ref, p1_ref, p2_ref, p3_ref)):
        for b in range(4):
            to_x = jnp.where(core == 0, (x + d) % 4, b)
            to_z = jnp.where(core == 0, b, (z + d) % 4)
            ref[b] = packed[to_x * 4 + to_z]


def pair_sum(keep, received):
    return call(
        pair_kernel,
        "pair_sum",
        (keep, received),
        [((4, 8, HALF), F32)] * 4,
        [VMEM((PLANE, 8, HALF), F32)],
    )


def line_sum_kernel(a_ref, b_ref, c_ref, d_ref, p0_ref, p1_ref, p2_ref, p3_ref, total):
    total[...] = (a_ref[...] + b_ref[...]) + (c_ref[...] + d_ref[...])
    x, z, core = place()
    own = jnp.where(core == 0, z, x)
    for e, ref in enumerate((p0_ref, p1_ref, p2_ref, p3_ref)):
        ref[...] = total[(own + e) % 4]


def line_sum(parts):
    return call(
        line_sum_kernel, "line_sum", parts, [((8, HALF), F32)] * 4, [VMEM((4, 8, HALF), F32)]
    )


def plane_kernel(a_ref, b_ref, c_ref, d_ref, out_ref):
    out_ref[...] = (a_ref[...] + b_ref[...]) + (c_ref[...] + d_ref[...])


def plane_sum(parts):
    return call(plane_kernel, "plane_sum", parts, [((8, HALF), F32)])[0]


def result_kernel(
    a_ref, b_ref, c_ref, d_ref, attn_ref, heads_ref, gain_ref, raw_ref, latent_ref, head_ref
):
    total = (a_ref[...] + b_ref[...]) + (c_ref[...] + d_ref[...])
    rest = D - HALF
    g_left, g_right = total[:OWN], total[OWN:, :rest]
    tot_row = total[OWN : OWN + 1, rest : rest + SIDE]
    sums = total[OWN:, rest + SIDE :]
    s_0 = sums[:, 0:1] * (1.0 / D)
    s_1 = sums[:, 1:2] * (1.0 / D)
    head = jnp.zeros((OWN, HEADS_LOCAL), F32)
    lane = lax.broadcasted_iota(jnp.int32, (OWN, HEADS_LOCAL), 1)
    for part, cols in ((g_left, slice(0, HALF)), (g_right, slice(HALF, D))):
        a_0 = attn_ref[:OWN, cols]
        vec = gain_ref[:, cols] * part - (s_0 * a_0 + s_1 * (attn_ref[OWN:, cols] - a_0))
        for h in range(HEADS_LOCAL):
            v = heads_ref[h, OWN:, cols] - heads_ref[h, :OWN, cols]
            dots = jnp.sum(vec * v, axis=1, keepdims=True)
            head = head + jnp.where(lane == h, dots, 0.0)
    head_ref[...] = head * (1.0 / (HEAD_DIM * STEPS))
    row = lax.broadcasted_iota(jnp.int32, (TOKENS, SIDE), 0)
    col = lax.broadcasted_iota(jnp.int32, (TOKENS, SIDE), 1)
    tot = jnp.sum(jnp.where(row == col, tot_row, 0.0), axis=1, keepdims=True)
    latent_ref[...] = raw_ref[...] * (1.0 / (tot * (1.0 / LAT) + EPSILON))


def result(parts, attn, heads, gain, raw):
    return call(
        result_kernel,
        "result",
        (*parts, attn, heads, gain, raw),
        [((TOKENS, LAT_LOCAL), F32), ((OWN, HEADS_LOCAL), F32)],
        final=True,
    )


def over_tp(x, order):
    others = [lax.ppermute(x, "tp", [(i, (i + d) % 4) for i in range(4)]) for d in order]
    return [x] + others


def send(x, stage, d):
    return lax.ppermute(x, "lat", shift(stage, d))


def swap(x):
    return lax.ppermute(x, "lat", CORE_SWAP)


def body(
    z_clean, z_corrupt, resid_clean, resid_corrupt, w_out, post_gain, w_enc, w_dec, cot, active
):
    heads, part = project(z_corrupt, z_clean, w_out)
    part, post_gain, resid_clean, resid_corrupt, w_enc, w_dec, cot, active = lax.optimization_barrier(
        (part, post_gain, resid_clean, resid_corrupt, w_enc, w_dec, cot, active)
    )
    gain = post_gain.reshape(1, D)
    resid = resid_project(resid_corrupt, resid_clean, w_enc)
    *parts, resid = lax.optimization_barrier((*over_tp(part, (3,1,2)), resid))
    attn, msg = norm(parts, resid_corrupt, resid_clean, gain)
    gf = grad_f(cot, w_dec, active)
    parts = [msg] + [send(msg, 0, d) for d in (3,2,1)]
    *parts, gf = lax.optimization_barrier((*parts, gf))
    block = line(parts)
    flipped = flip(w_enc)
    blocks = [block] + [send(block, 1, e) for e in (1, 2, 3)]
    blocks[2], flipped = lax.optimization_barrier((blocks[2], flipped))
    others = [swap(b) for b in blocks]
    *blocks, others[2] = lax.optimization_barrier((*blocks, others[2]))
    pre_own, side = own_project(blocks, w_enc)
    raw, keep, give = latents(others, side, pre_own, resid, gf, w_enc, flipped)
    parts = pair_sum(keep, swap(give))
    parts = line_sum([parts[0]] + [send(parts[d], 0, d) for d in (2,1,3)])
    total = plane_sum([parts[0]] + [send(parts[e], 1, e) for e in (2,1,3)])
    return tuple(result(over_tp(total, (3,1,2)), attn, heads, gain, raw))


def solution(mesh):
    placed = (
        P(None, "tp"),
        P(None, "tp"),
        P(),
        P(),
        P("tp", None),
        P(),
        P(None, ("lat", "tp")),
        P(("lat", "tp"), None),
        P(),
        P(None, ("lat", "tp")),
    )
    return jax.shard_map(
        body,
        mesh=mesh,
        in_specs=placed,
        out_specs=(P(None, ("lat", "tp")), P("lat", "tp")),
        check_vma=False,
    )
```

```python
import jax
import jax.numpy as jnp
from jax import lax
from jax.experimental import pallas as pl
from jax.experimental.pallas import tpu as pltpu
from jax.sharding import PartitionSpec as P

D = 3584
TOKENS = 128
STEPS = 4
HEAD_DIM = 256
HEADS_LOCAL = 4
LAT = 131072
LAT_LOCAL = 1024
EPSILON = 1e-06
OWN = 4
PLANE = 16
SIDE = 128
MSG = D + SIDE
RED = D + 2 * SIDE
HALF = RED // 2
ALPHAS = tuple(k / 3.0 for k in range(STEPS))
F32 = jnp.float32
BF16 = jnp.bfloat16
VMEM = pltpu.VMEM
MIB = 1024 * 1024


def lat_index(x, z, core):
    return ((x % 4) * 4 + z % 4) * 2 + core


def shift(stage, d):
    pairs = []
    for x in range(4):
        for z in range(4):
            for core in range(2):
                along_x = (stage == 0) == (core == 0)
                to = (x + d, z) if along_x else (x, z + d)
                pairs.append((lat_index(x, z, core), lat_index(*to, core)))
    return pairs


CORE_SWAP = [(i, i ^ 1) for i in range(32)]


def place():
    index = lax.axis_index("lat")
    return index // 8, (index // 2) % 4, index % 2


def call(kernel, name, operands, outs, scratch=(), mib=8, flops=10**6, hbm=(), final=False):
    spaces = [pltpu.HBM if i in hbm else VMEM for i in range(len(operands))]
    nbytes = sum(x.size * x.dtype.itemsize for x in operands)
    return pl.pallas_call(
        kernel,
        in_specs=[pl.BlockSpec(memory_space=s) for s in spaces],
        out_specs=[pl.BlockSpec(memory_space=VMEM)] * len(outs),
        out_shape=[(jax.ShapeDtypeStruct if final else VMEM)(shape, dtype) for shape, dtype in outs],
        scratch_shapes=list(scratch),
        compiler_params=pltpu.CompilerParams(vmem_limit_bytes=mib * MIB),
        cost_estimate=pl.CostEstimate(flops=flops, bytes_accessed=nbytes, transcendentals=0),
        name=name,
    )(*[pltpu.with_memory_space_constraint(x, s) for x, s in zip(operands, spaces)])


def nt(a, b):
    return lax.dot_general(a, b, (((1,), (1,)), ((), ())), preferred_element_type=F32)


def nn(a, b):
    return lax.dot_general(a, b, (((1,), (0,)), ((), ())), preferred_element_type=F32)


def project_kernel(zc_ref, zn_ref, w_ref, heads_ref, part_ref, z_s, w_s, z_sems, sems):
    index = lax.axis_index("lat")
    block = pl.ds(pl.multiple_of((index // 4) * 16, 16), 16)
    z_copies = [
        pltpu.make_async_copy(ref.at[block, :], z_s.at[i], z_sems.at[i])
        for i, ref in enumerate((zc_ref, zn_ref))
    ]
    for copy in z_copies:
        copy.start()
    copies = []
    for i in range(2):
        rows = pl.ds(i * 2 * HEAD_DIM, 2 * HEAD_DIM)
        copies.append(pltpu.make_async_copy(w_ref.at[rows, :], w_s.at[rows, :], sems.at[i]))
        copies[-1].start()
    first = (index % 4) * OWN
    row = lax.broadcasted_iota(jnp.int32, (16, 16), 0)
    token = lax.broadcasted_iota(jnp.int32, (16, 16), 1)
    pick_c = ((row < OWN) & (token == first + row)).astype(F32).astype(BF16)
    pick_n = ((row >= OWN) & (row < 2 * OWN) & (token == first + row - OWN)).astype(F32).astype(BF16)
    for copy in z_copies:
        copy.wait()
    z = (nn(pick_c, z_s[0]) + nn(pick_n, z_s[1])).astype(BF16)
    for h in range(HEADS_LOCAL):
        if h % 2 == 0:
            copies[h // 2].wait()
        cols = slice(h * HEAD_DIM, (h + 1) * HEAD_DIM)
        out = nn(z[:, cols], w_s[cols, :])[: 2 * OWN]
        heads_ref[h] = out
        if h == 0:
            part_ref[...] = out
        else:
            part_ref[...] += out


def project(z_corrupt, z_clean, w_out):
    return call(
        project_kernel,
        "project",
        (z_corrupt, z_clean, w_out),
        [((HEADS_LOCAL, 2 * OWN, D), F32), ((2 * OWN, D), F32)],
        [
            VMEM((2, 16, 1024), BF16),
            VMEM((1024, D), BF16),
            pltpu.SemaphoreType.DMA((2,)),
            pltpu.SemaphoreType.DMA((2,)),
        ],
        mib=12,
        flops=2 * 16 * 1024 * D,
        hbm=(0, 1, 2),
    )


def grad_f_kernel(cot_ref, w_ref, active_ref, out_ref, rows, acc):
    rows[...] = cot_ref[...].reshape(TOKENS * STEPS, D)
    for n in range(w_ref.shape[0] // acc.shape[0] // SIDE):
        base = n * acc.shape[0] * SIDE
        out = nt(rows[...], w_ref[base : base + acc.shape[0] * SIDE, :])
        for j in range(acc.shape[0]):
            acc[j] = out[:, j * SIDE : (j + 1) * SIDE]
            cols = slice(base + j * SIDE, base + (j + 1) * SIDE)
            act = active_ref[:, cols].astype(F32)
            for k in range(STEPS):
                out_ref[k, :, cols] = act * acc[j, pl.ds(k, TOKENS, stride=STEPS), :]


def grad_f(cot, w_dec, active):
    return call(
        grad_f_kernel,
        "grad_f",
        (cot, w_dec, active),
        [((STEPS, TOKENS, LAT_LOCAL), F32)],
        [VMEM((TOKENS * STEPS, D), BF16), VMEM((2, TOKENS * STEPS, SIDE), F32)],
        mib=8,
        flops=2 * 512 * 1024 * D,
    )[0]


def norm_kernel(a_ref, b_ref, c_ref, d_ref, rc_ref, rn_ref, gain_ref, attn_ref, msg_ref):
    attn = (a_ref[...] + b_ref[...]) + (c_ref[...] + d_ref[...])
    attn_ref[...] = attn
    first = lax.axis_index("lat") * OWN
    row = lax.broadcasted_iota(jnp.int32, (16, TOKENS), 0)
    token = lax.broadcasted_iota(jnp.int32, (16, TOKENS), 1)
    pick = ((row < 2 * OWN) & (token == first + row % OWN)).astype(F32).astype(BF16)
    corrupt = nn(pick, rc_ref[...])[: 2 * OWN]
    clean = nn(pick, rn_ref[...])[: 2 * OWN]
    upper = lax.broadcasted_iota(jnp.int32, (2 * OWN, D), 0) >= OWN
    resid = jnp.where(upper, corrupt + (clean - corrupt), corrupt)
    other = pltpu.roll(attn, OWN, 0)
    a_0 = jnp.where(upper, other, attn)
    delta = jnp.where(upper, attn, other) - a_0
    lane = lax.broadcasted_iota(jnp.int32, (2 * OWN, SIDE), 1)
    side = jnp.zeros((2 * OWN, SIDE), F32)
    invs = []
    for k in range(STEPS):
        a_k = a_0 + ALPHAS[k] * delta
        inv = lax.rsqrt(jnp.sum(a_k * a_k, axis=1, keepdims=True) * (1.0 / D) + EPSILON)
        invs.append(inv)
        side = jnp.where(lane == k, inv, side)
    low = lax.broadcasted_iota(jnp.int32, (2 * OWN, 1), 0) < OWN
    own_inv = jnp.where(low, invs[0], invs[3])
    sae_in = resid + attn * own_inv * gain_ref[...]
    msg_ref[:, :D] = sae_in
    msg_ref[:, D:] = side


def norm(parts, resid_corrupt, resid_clean, gain):
    return call(
        norm_kernel,
        "norm",
        (*parts, resid_corrupt, resid_clean, gain),
        [((2 * OWN, D), F32), ((2 * OWN, MSG), F32)],
    )


def line_kernel(a_ref, b_ref, c_ref, d_ref, out_ref):
    for d, ref in zip((0, *(3,2,1)), (a_ref, b_ref, c_ref, d_ref)):
        out_ref[d] = ref[...]


def line(parts):
    return call(line_kernel, "line", parts, [((4, 2 * OWN, MSG), F32)])[0]


def assemble(refs, core, out):
    x, z, _ = place()
    for e, ref in enumerate(refs):
        for d in range(4):
            from_x = (x + 4 - jnp.where(core == 0, d, e)) % 4
            from_z = (z + 4 - jnp.where(core == 0, e, d)) % 4
            out[from_x * 4 + from_z] = ref[d]


def flip_kernel(w_ref, out_ref):
    out_ref[...] = w_ref[...].T


def flip(w_enc):
    return call(flip_kernel, "flip", (w_enc,), [((LAT_LOCAL, D), BF16)])[0]


def resid_kernel(rc_ref, rn_ref, w_ref, out_ref):
    out_ref[0] = nn(rc_ref[...], w_ref[...])
    out_ref[1] = nn(rn_ref[...], w_ref[...])


def resid_project(resid_corrupt, resid_clean, w_enc):
    return call(
        resid_kernel,
        "resid_project",
        (resid_corrupt, resid_clean, w_enc),
        [((2, TOKENS, LAT_LOCAL), F32)],
        flops=2 * 256 * 1024 * D,
    )[0]


def own_kernel(a_ref, b_ref, c_ref, d_ref, w_ref, out_ref, side_ref, rows):
    assemble((a_ref, b_ref, c_ref, d_ref), place()[2], rows)
    side_ref[...] = rows[:, :, D:]
    out_ref[...] = nn(rows[:, :, :D].reshape(TOKENS, D).astype(BF16), w_ref[...])


def own_project(blocks, w_enc):
    return call(
        own_kernel,
        "own_project",
        (*blocks, w_enc),
        [((TOKENS, LAT_LOCAL), F32), ((PLANE, 2 * OWN, SIDE), F32)],
        [VMEM((PLANE, 2 * OWN, MSG), F32)],
        flops=2 * 128 * 1024 * D,
    )


def upper_rows(width):
    return lax.broadcasted_iota(jnp.int32, (TOKENS, width), 0) % 8 >= OWN


def swap_rows(x):
    width = x.shape[-1]
    return pltpu.roll(x.reshape(PLANE, 8, width), OWN, 1).reshape(TOKENS, width)


def by_step(own, other, core):
    up = upper_rows(own.shape[-1])
    is_0 = core == 0
    x_0 = jnp.where(is_0, own, other)
    x_1 = jnp.where(is_0, other, own)
    return jnp.where(up, swap_rows(x_1), x_0), jnp.where(up, x_1, swap_rows(x_0))


def by_core(x, core):
    width = x.shape[-1]
    pairs = x.reshape(PLANE // 2, 2, 8, width)
    even, odd = pairs[:, 0], pairs[:, 1]
    up = lax.broadcasted_iota(jnp.int32, even.shape, 1) >= OWN
    core_0 = jnp.where(up, pltpu.roll(odd, OWN, 1), even).reshape(TOKENS // 2, width)
    core_1 = jnp.where(up, odd, pltpu.roll(even, OWN, 1)).reshape(TOKENS // 2, width)
    is_0 = core == 0
    return jnp.where(is_0, core_0, core_1), jnp.where(is_0, core_1, core_0)


def lane_fold(x):
    total = x[:, :SIDE]
    for start in range(SIDE, x.shape[1], SIDE):
        total = total + x[:, start : start + SIDE]
    return total


def latents_kernel(
    a_ref, b_ref, c_ref, d_ref, side_ref, pre_ref, resid_ref, gf_ref, w_ref, flip_ref,
    raw_ref, keep_ref, send_ref,
    other, pre_s, hidden_s, inv_s,
):
    core = place()[2]
    assemble((a_ref, b_ref, c_ref, d_ref), 1 - core, other)
    pre_s[...] = nn(other[:, :, :D].reshape(TOKENS, D).astype(BF16), w_ref[...])
    side = by_step(
        side_ref[...].reshape(TOKENS, SIDE), other[:, :, D:].reshape(TOKENS, SIDE), core
    )[0]
    for k in range(STEPS):
        inv = jnp.broadcast_to(side[:, k : k + 1], (TOKENS, SIDE))
        inv_s[k] = inv
        inv_s[STEPS + k] = inv * inv * inv
    for k, j in ((0, 2 * STEPS), (STEPS - 1, 2 * STEPS + 1)):
        inv_s[j] = 1.0 / inv_s[k]
    tot = jnp.zeros((TOKENS, SIDE), F32)
    s_0 = jnp.zeros((TOKENS, SIDE), F32)
    s_1 = jnp.zeros((TOKENS, SIDE), F32)
    half = TOKENS // 2
    for start in range(0, LAT_LOCAL, SIDE):
        cols = slice(start, start + SIDE)
        pre_0, pre_3 = by_step(pre_ref[:, cols], pre_s[:, cols], core)
        gf = [gf_ref[k, :, cols] for k in range(STEPS)]
        raw = (pre_3 - pre_0) * (((gf[0] + gf[1]) + (gf[2] + gf[3])) * 0.25)
        raw_ref[:, cols] = raw
        tot = tot + jnp.abs(raw)
        q_0 = (pre_0 - resid_ref[0, :, cols]) * inv_s[2 * STEPS]
        q_d = (pre_3 - resid_ref[1, :, cols]) * inv_s[2 * STEPS + 1] - q_0
        u = [inv_s[STEPS + k] * gf[k] for k in range(STEPS)]
        sum_0 = (u[0] + u[1]) + (u[2] + u[3])
        sum_1 = ALPHAS[1] * u[1] + (ALPHAS[2] * u[2] + u[3])
        sum_2 = ALPHAS[1] ** 2 * u[1] + (ALPHAS[2] ** 2 * u[2] + u[3])
        s_0 = s_0 + (sum_0 * q_0 + sum_1 * q_d)
        s_1 = s_1 + (sum_1 * q_0 + sum_2 * q_d)
        hidden = (inv_s[0] * gf[0] + inv_s[1] * gf[1]) + (inv_s[2] * gf[2] + inv_s[3] * gf[3])
        first, second = by_core(hidden, core)
        hidden_s[:half, cols] = first.astype(BF16)
        hidden_s[half:, cols] = second.astype(BF16)
    grad = nn(hidden_s[...], flip_ref[...])
    keep_ref[:, :D] = grad[:half]
    send_ref[:, :D] = grad[half:]
    row = lax.broadcasted_iota(jnp.int32, (TOKENS, SIDE), 0)
    lane = lax.broadcasted_iota(jnp.int32, (TOKENS, SIDE), 1)
    tot = jnp.sum(tot, axis=1, keepdims=True)
    tot_row = jnp.sum(jnp.where(row == lane, tot, 0.0), axis=0, keepdims=True)
    tot_all = jnp.broadcast_to(tot_row, (half, SIDE))
    s_0 = jnp.sum(s_0, axis=1, keepdims=True)
    s_1 = jnp.sum(s_1, axis=1, keepdims=True)
    first, second = by_core(jnp.where(lane == 0, s_0, jnp.where(lane == 1, s_1, 0.0)), core)
    keep_ref[:, D : D + SIDE] = tot_all
    send_ref[:, D : D + SIDE] = tot_all
    keep_ref[:, D + SIDE :] = first
    send_ref[:, D + SIDE :] = second


def latents(others, side, pre_own, resid, gf, w_enc, flipped):
    half = TOKENS // 2
    return call(
        latents_kernel,
        "latents",
        (*others, side, pre_own, resid, gf, w_enc, flipped),
        [((TOKENS, LAT_LOCAL), F32), ((half, RED), F32), ((half, RED), F32)],
        [
            VMEM((PLANE, 2 * OWN, MSG), F32),
            VMEM((TOKENS, LAT_LOCAL), F32),
            VMEM((TOKENS, LAT_LOCAL), BF16),
            VMEM((2 * STEPS + 2, TOKENS, SIDE), F32),
        ],
        flops=4 * 128 * 1024 * D,
    )


def pair_kernel(a_ref, b_ref, p0_ref, p1_ref, p2_ref, p3_ref, packed):
    up = lax.broadcasted_iota(jnp.int32, (8, HALF), 0) >= OWN
    for g in range(PLANE // 2):
        tile = a_ref[8 * g : 8 * g + 8, :] + b_ref[8 * g : 8 * g + 8, :]
        left, right = tile[:, :HALF], tile[:, HALF:]
        packed[2 * g] = jnp.where(up, pltpu.roll(right, OWN, 0), left)
        packed[2 * g + 1] = jnp.where(up, right, pltpu.roll(left, OWN, 0))
    x, z, core = place()
    for d, ref in enumerate((p0_ref, p1_ref, p2_ref, p3_ref)):
        for b in range(4):
            to_x = jnp.where(core == 0, (x + d) % 4, b)
            to_z = jnp.where(core == 0, b, (z + d) % 4)
            ref[b] = packed[to_x * 4 + to_z]


def pair_sum(keep, received):
    return call(
        pair_kernel,
        "pair_sum",
        (keep, received),
        [((4, 8, HALF), F32)] * 4,
        [VMEM((PLANE, 8, HALF), F32)],
    )


def line_sum_kernel(a_ref, b_ref, c_ref, d_ref, p0_ref, p1_ref, p2_ref, p3_ref, total):
    total[...] = (a_ref[...] + b_ref[...]) + (c_ref[...] + d_ref[...])
    x, z, core = place()
    own = jnp.where(core == 0, z, x)
    for e, ref in enumerate((p0_ref, p1_ref, p2_ref, p3_ref)):
        ref[...] = total[(own + e) % 4]


def line_sum(parts):
    return call(
        line_sum_kernel, "line_sum", parts, [((8, HALF), F32)] * 4, [VMEM((4, 8, HALF), F32)]
    )


def plane_kernel(a_ref, b_ref, c_ref, d_ref, out_ref):
    out_ref[...] = (a_ref[...] + b_ref[...]) + (c_ref[...] + d_ref[...])


def plane_sum(parts):
    return call(plane_kernel, "plane_sum", parts, [((8, HALF), F32)])[0]


def result_kernel(
    a_ref, b_ref, c_ref, d_ref, attn_ref, heads_ref, gain_ref, raw_ref, latent_ref, head_ref
):
    total = (a_ref[...] + b_ref[...]) + (c_ref[...] + d_ref[...])
    rest = D - HALF
    g_left, g_right = total[:OWN], total[OWN:, :rest]
    tot_row = total[OWN : OWN + 1, rest : rest + SIDE]
    sums = total[OWN:, rest + SIDE :]
    s_0 = sums[:, 0:1] * (1.0 / D)
    s_1 = sums[:, 1:2] * (1.0 / D)
    head = jnp.zeros((OWN, HEADS_LOCAL), F32)
    lane = lax.broadcasted_iota(jnp.int32, (OWN, HEADS_LOCAL), 1)
    for part, cols in ((g_left, slice(0, HALF)), (g_right, slice(HALF, D))):
        a_0 = attn_ref[:OWN, cols]
        vec = gain_ref[:, cols] * part - (s_0 * a_0 + s_1 * (attn_ref[OWN:, cols] - a_0))
        for h in range(HEADS_LOCAL):
            v = heads_ref[h, OWN:, cols] - heads_ref[h, :OWN, cols]
            dots = jnp.sum(vec * v, axis=1, keepdims=True)
            head = head + jnp.where(lane == h, dots, 0.0)
    head_ref[...] = head * (1.0 / (HEAD_DIM * STEPS))
    row = lax.broadcasted_iota(jnp.int32, (TOKENS, SIDE), 0)
    col = lax.broadcasted_iota(jnp.int32, (TOKENS, SIDE), 1)
    tot = jnp.sum(jnp.where(row == col, tot_row, 0.0), axis=1, keepdims=True)
    latent_ref[...] = raw_ref[...] * (1.0 / (tot * (1.0 / LAT) + EPSILON))


def result(parts, attn, heads, gain, raw):
    return call(
        result_kernel,
        "result",
        (*parts, attn, heads, gain, raw),
        [((TOKENS, LAT_LOCAL), F32), ((OWN, HEADS_LOCAL), F32)],
        final=True,
    )


def over_tp(x, order):
    others = [lax.ppermute(x, "tp", [(i, (i + d) % 4) for i in range(4)]) for d in order]
    return [x] + others


def send(x, stage, d):
    return lax.ppermute(x, "lat", shift(stage, d))


def swap(x):
    return lax.ppermute(x, "lat", CORE_SWAP)


def body(
    z_clean, z_corrupt, resid_clean, resid_corrupt, w_out, post_gain, w_enc, w_dec, cot, active
):
    heads, part = project(z_corrupt, z_clean, w_out)
    part, post_gain, resid_clean, resid_corrupt, w_enc, w_dec, cot, active = lax.optimization_barrier(
        (part, post_gain, resid_clean, resid_corrupt, w_enc, w_dec, cot, active)
    )
    gain = post_gain.reshape(1, D)
    resid = resid_project(resid_corrupt, resid_clean, w_enc)
    *parts, resid = lax.optimization_barrier((*over_tp(part, (3,1,2)), resid))
    attn, msg = norm(parts, resid_corrupt, resid_clean, gain)
    gf = grad_f(cot, w_dec, active)
    parts = [msg] + [send(msg, 0, d) for d in (3,2,1)]
    *parts, gf = lax.optimization_barrier((*parts, gf))
    block = line(parts)
    flipped = flip(w_enc)
    blocks = [block] + [send(block, 1, e) for e in (1, 2, 3)]
    first = swap(block)
    blocks[1], flipped, first = lax.optimization_barrier((blocks[1], flipped, first))
    others = [first] + [swap(b) for b in blocks[1:]]
    *blocks, others[1] = lax.optimization_barrier((*blocks, others[1]))
    pre_own, side = own_project(blocks, w_enc)
    raw, keep, give = latents(others, side, pre_own, resid, gf, w_enc, flipped)
    parts = pair_sum(keep, swap(give))
    parts = line_sum([parts[0]] + [send(parts[d], 0, d) for d in (2,1,3)])
    total = plane_sum([parts[0]] + [send(parts[e], 1, e) for e in (2,1,3)])
    return tuple(result(over_tp(total, (3,1,2)), attn, heads, gain, raw))


def solution(mesh):
    placed = (
        P(None, "tp"),
        P(None, "tp"),
        P(),
        P(),
        P("tp", None),
        P(),
        P(None, ("lat", "tp")),
        P(("lat", "tp"), None),
        P(),
        P(None, ("lat", "tp")),
    )
    return jax.shard_map(
        body,
        mesh=mesh,
        in_specs=placed,
        out_specs=(P(None, ("lat", "tp")), P("lat", "tp")),
        check_vma=False,
    )
```

```python
import jax
import jax.numpy as jnp
from jax import lax
from jax.experimental import pallas as pl
from jax.experimental.pallas import tpu as pltpu
from jax.sharding import PartitionSpec as P

D = 3584
TOKENS = 128
STEPS = 4
HEAD_DIM = 256
HEADS_LOCAL = 4
LAT = 131072
LAT_LOCAL = 1024
EPSILON = 1e-06
OWN = 4
PLANE = 16
SIDE = 128
MSG = D + SIDE
RED = D + 2 * SIDE
HALF = RED // 2
ALPHAS = tuple(k / 3.0 for k in range(STEPS))
F32 = jnp.float32
BF16 = jnp.bfloat16
VMEM = pltpu.VMEM
MIB = 1024 * 1024


def lat_index(x, z, core):
    return ((x % 4) * 4 + z % 4) * 2 + core


def shift(stage, d):
    pairs = []
    for x in range(4):
        for z in range(4):
            for core in range(2):
                along_x = (stage == 0) == (core == 0)
                to = (x + d, z) if along_x else (x, z + d)
                pairs.append((lat_index(x, z, core), lat_index(*to, core)))
    return pairs


CORE_SWAP = [(i, i ^ 1) for i in range(32)]


def place():
    index = lax.axis_index("lat")
    return index // 8, (index // 2) % 4, index % 2


def call(kernel, name, operands, outs, scratch=(), mib=8, flops=10**6, hbm=(), final=False):
    spaces = [pltpu.HBM if i in hbm else VMEM for i in range(len(operands))]
    nbytes = sum(x.size * x.dtype.itemsize for x in operands)
    return pl.pallas_call(
        kernel,
        in_specs=[pl.BlockSpec(memory_space=s) for s in spaces],
        out_specs=[pl.BlockSpec(memory_space=VMEM)] * len(outs),
        out_shape=[(jax.ShapeDtypeStruct if final else VMEM)(shape, dtype) for shape, dtype in outs],
        scratch_shapes=list(scratch),
        compiler_params=pltpu.CompilerParams(vmem_limit_bytes=mib * MIB),
        cost_estimate=pl.CostEstimate(flops=flops, bytes_accessed=nbytes, transcendentals=0),
        name=name,
    )(*[pltpu.with_memory_space_constraint(x, s) for x, s in zip(operands, spaces)])


def nt(a, b):
    return lax.dot_general(a, b, (((1,), (1,)), ((), ())), preferred_element_type=F32)


def nn(a, b):
    return lax.dot_general(a, b, (((1,), (0,)), ((), ())), preferred_element_type=F32)


def project_kernel(zc_ref, zn_ref, w_ref, heads_ref, part_ref, z_s, w_s, z_sems, sems):
    index = lax.axis_index("lat")
    block = pl.ds(pl.multiple_of((index // 4) * 16, 16), 16)
    z_copies = [
        pltpu.make_async_copy(ref.at[block, :], z_s.at[i], z_sems.at[i])
        for i, ref in enumerate((zc_ref, zn_ref))
    ]
    for copy in z_copies:
        copy.start()
    copies = []
    for i in range(2):
        rows = pl.ds(i * 2 * HEAD_DIM, 2 * HEAD_DIM)
        copies.append(pltpu.make_async_copy(w_ref.at[rows, :], w_s.at[rows, :], sems.at[i]))
        copies[-1].start()
    first = (index % 4) * OWN
    row = lax.broadcasted_iota(jnp.int32, (16, 16), 0)
    token = lax.broadcasted_iota(jnp.int32, (16, 16), 1)
    pick_c = ((row < OWN) & (token == first + row)).astype(F32).astype(BF16)
    pick_n = ((row >= OWN) & (row < 2 * OWN) & (token == first + row - OWN)).astype(F32).astype(BF16)
    for copy in z_copies:
        copy.wait()
    z = (nn(pick_c, z_s[0]) + nn(pick_n, z_s[1])).astype(BF16)
    for h in range(HEADS_LOCAL):
        if h % 2 == 0:
            copies[h // 2].wait()
        cols = slice(h * HEAD_DIM, (h + 1) * HEAD_DIM)
        out = nn(z[:, cols], w_s[cols, :])[: 2 * OWN]
        heads_ref[h] = out
        if h == 0:
            part_ref[...] = out
        else:
            part_ref[...] += out


def project(z_corrupt, z_clean, w_out):
    return call(
        project_kernel,
        "project",
        (z_corrupt, z_clean, w_out),
        [((HEADS_LOCAL, 2 * OWN, D), F32), ((2 * OWN, D), F32)],
        [
            VMEM((2, 16, 1024), BF16),
            VMEM((1024, D), BF16),
            pltpu.SemaphoreType.DMA((2,)),
            pltpu.SemaphoreType.DMA((2,)),
        ],
        mib=12,
        flops=2 * 16 * 1024 * D,
        hbm=(0, 1, 2),
    )


def grad_f_kernel(cot_ref, w_ref, active_ref, out_ref, rows, acc):
    rows[...] = cot_ref[...].reshape(TOKENS * STEPS, D)
    for n in range(w_ref.shape[0] // acc.shape[0] // SIDE):
        base = n * acc.shape[0] * SIDE
        out = nt(rows[...], w_ref[base : base + acc.shape[0] * SIDE, :])
        for j in range(acc.shape[0]):
            acc[j] = out[:, j * SIDE : (j + 1) * SIDE]
            cols = slice(base + j * SIDE, base + (j + 1) * SIDE)
            act = active_ref[:, cols].astype(F32)
            for k in range(STEPS):
                out_ref[k, :, cols] = act * acc[j, pl.ds(k, TOKENS, stride=STEPS), :]


def grad_f(cot, w_dec, active):
    return call(
        grad_f_kernel,
        "grad_f",
        (cot, w_dec, active),
        [((STEPS, TOKENS, LAT_LOCAL), F32)],
        [VMEM((TOKENS * STEPS, D), BF16), VMEM((2, TOKENS * STEPS, SIDE), F32)],
        mib=8,
        flops=2 * 512 * 1024 * D,
    )[0]


def norm_kernel(a_ref, b_ref, c_ref, d_ref, rc_ref, rn_ref, gain_ref, attn_ref, msg_ref):
    attn = (a_ref[...] + b_ref[...]) + (c_ref[...] + d_ref[...])
    attn_ref[...] = attn
    first = lax.axis_index("lat") * OWN
    row = lax.broadcasted_iota(jnp.int32, (16, TOKENS), 0)
    token = lax.broadcasted_iota(jnp.int32, (16, TOKENS), 1)
    pick = ((row < 2 * OWN) & (token == first + row % OWN)).astype(F32).astype(BF16)
    corrupt = nn(pick, rc_ref[...])[: 2 * OWN]
    clean = nn(pick, rn_ref[...])[: 2 * OWN]
    upper = lax.broadcasted_iota(jnp.int32, (2 * OWN, D), 0) >= OWN
    resid = jnp.where(upper, corrupt + (clean - corrupt), corrupt)
    other = pltpu.roll(attn, OWN, 0)
    a_0 = jnp.where(upper, other, attn)
    delta = jnp.where(upper, attn, other) - a_0
    lane = lax.broadcasted_iota(jnp.int32, (2 * OWN, SIDE), 1)
    side = jnp.zeros((2 * OWN, SIDE), F32)
    invs = []
    for k in range(STEPS):
        a_k = a_0 + ALPHAS[k] * delta
        inv = lax.rsqrt(jnp.sum(a_k * a_k, axis=1, keepdims=True) * (1.0 / D) + EPSILON)
        invs.append(inv)
        side = jnp.where(lane == k, inv, side)
    low = lax.broadcasted_iota(jnp.int32, (2 * OWN, 1), 0) < OWN
    own_inv = jnp.where(low, invs[0], invs[3])
    sae_in = resid + attn * own_inv * gain_ref[...]
    msg_ref[:, :D] = sae_in
    msg_ref[:, D:] = side


def norm(parts, resid_corrupt, resid_clean, gain):
    return call(
        norm_kernel,
        "norm",
        (*parts, resid_corrupt, resid_clean, gain),
        [((2 * OWN, D), F32), ((2 * OWN, MSG), F32)],
    )


def line_kernel(a_ref, b_ref, c_ref, d_ref, out_ref):
    for d, ref in zip((0, *(2, 3, 1)), (a_ref, b_ref, c_ref, d_ref)):
        out_ref[d] = ref[...]


def line(parts):
    return call(line_kernel, "line", parts, [((4, 2 * OWN, MSG), F32)])[0]


def assemble(refs, core, out):
    x, z, _ = place()
    for e, ref in enumerate(refs):
        for d in range(4):
            from_x = (x + 4 - jnp.where(core == 0, d, e)) % 4
            from_z = (z + 4 - jnp.where(core == 0, e, d)) % 4
            out[from_x * 4 + from_z] = ref[d]


def flip_kernel(w_ref, out_ref):
    out_ref[...] = w_ref[...].T


def flip(w_enc):
    return call(flip_kernel, "flip", (w_enc,), [((LAT_LOCAL, D), BF16)])[0]


def resid_kernel(rc_ref, rn_ref, w_ref, out_ref):
    out_ref[0] = nn(rc_ref[...], w_ref[...])
    out_ref[1] = nn(rn_ref[...], w_ref[...])


def resid_project(resid_corrupt, resid_clean, w_enc):
    return call(
        resid_kernel,
        "resid_project",
        (resid_corrupt, resid_clean, w_enc),
        [((2, TOKENS, LAT_LOCAL), F32)],
        flops=2 * 256 * 1024 * D,
    )[0]


def own_kernel(a_ref, b_ref, c_ref, d_ref, w_ref, out_ref, side_ref, rows):
    assemble((a_ref, b_ref, c_ref, d_ref), place()[2], rows)
    side_ref[...] = rows[:, :, D:]
    out_ref[...] = nn(rows[:, :, :D].reshape(TOKENS, D).astype(BF16), w_ref[...])


def own_project(blocks, w_enc):
    return call(
        own_kernel,
        "own_project",
        (*blocks, w_enc),
        [((TOKENS, LAT_LOCAL), F32), ((PLANE, 2 * OWN, SIDE), F32)],
        [VMEM((PLANE, 2 * OWN, MSG), F32)],
        flops=2 * 128 * 1024 * D,
    )


def upper_rows(width):
    return lax.broadcasted_iota(jnp.int32, (TOKENS, width), 0) % 8 >= OWN


def swap_rows(x):
    width = x.shape[-1]
    return pltpu.roll(x.reshape(PLANE, 8, width), OWN, 1).reshape(TOKENS, width)


def by_step(own, other, core):
    up = upper_rows(own.shape[-1])
    is_0 = core == 0
    x_0 = jnp.where(is_0, own, other)
    x_1 = jnp.where(is_0, other, own)
    return jnp.where(up, swap_rows(x_1), x_0), jnp.where(up, x_1, swap_rows(x_0))


def by_core(x, core):
    width = x.shape[-1]
    pairs = x.reshape(PLANE // 2, 2, 8, width)
    even, odd = pairs[:, 0], pairs[:, 1]
    up = lax.broadcasted_iota(jnp.int32, even.shape, 1) >= OWN
    core_0 = jnp.where(up, pltpu.roll(odd, OWN, 1), even).reshape(TOKENS // 2, width)
    core_1 = jnp.where(up, odd, pltpu.roll(even, OWN, 1)).reshape(TOKENS // 2, width)
    is_0 = core == 0
    return jnp.where(is_0, core_0, core_1), jnp.where(is_0, core_1, core_0)


def lane_fold(x):
    total = x[:, :SIDE]
    for start in range(SIDE, x.shape[1], SIDE):
        total = total + x[:, start : start + SIDE]
    return total


def latents_kernel(
    a_ref, b_ref, c_ref, d_ref, side_ref, pre_ref, resid_ref, gf_ref, w_ref, flip_ref,
    raw_ref, keep_ref, send_ref,
    other, pre_s, hidden_s, inv_s,
):
    core = place()[2]
    assemble((a_ref, b_ref, c_ref, d_ref), 1 - core, other)
    pre_s[...] = nn(other[:, :, :D].reshape(TOKENS, D).astype(BF16), w_ref[...])
    side = by_step(
        side_ref[...].reshape(TOKENS, SIDE), other[:, :, D:].reshape(TOKENS, SIDE), core
    )[0]
    for k in range(STEPS):
        inv = jnp.broadcast_to(side[:, k : k + 1], (TOKENS, SIDE))
        inv_s[k] = inv
        inv_s[STEPS + k] = inv * inv * inv
    for k, j in ((0, 2 * STEPS), (STEPS - 1, 2 * STEPS + 1)):
        inv_s[j] = 1.0 / inv_s[k]
    tot = jnp.zeros((TOKENS, SIDE), F32)
    s_0 = jnp.zeros((TOKENS, SIDE), F32)
    s_1 = jnp.zeros((TOKENS, SIDE), F32)
    half = TOKENS // 2
    for start in range(0, LAT_LOCAL, SIDE):
        cols = slice(start, start + SIDE)
        pre_0, pre_3 = by_step(pre_ref[:, cols], pre_s[:, cols], core)
        gf = [gf_ref[k, :, cols] for k in range(STEPS)]
        raw = (pre_3 - pre_0) * (((gf[0] + gf[1]) + (gf[2] + gf[3])) * 0.25)
        raw_ref[:, cols] = raw
        tot = tot + jnp.abs(raw)
        q_0 = (pre_0 - resid_ref[0, :, cols]) * inv_s[2 * STEPS]
        q_d = (pre_3 - resid_ref[1, :, cols]) * inv_s[2 * STEPS + 1] - q_0
        u = [inv_s[STEPS + k] * gf[k] for k in range(STEPS)]
        sum_0 = (u[0] + u[1]) + (u[2] + u[3])
        sum_1 = ALPHAS[1] * u[1] + (ALPHAS[2] * u[2] + u[3])
        sum_2 = ALPHAS[1] ** 2 * u[1] + (ALPHAS[2] ** 2 * u[2] + u[3])
        s_0 = s_0 + (sum_0 * q_0 + sum_1 * q_d)
        s_1 = s_1 + (sum_1 * q_0 + sum_2 * q_d)
        hidden = (inv_s[0] * gf[0] + inv_s[1] * gf[1]) + (inv_s[2] * gf[2] + inv_s[3] * gf[3])
        first, second = by_core(hidden, core)
        hidden_s[:half, cols] = first.astype(BF16)
        hidden_s[half:, cols] = second.astype(BF16)
    grad = nn(hidden_s[...], flip_ref[...])
    keep_ref[:, :D] = grad[:half]
    send_ref[:, :D] = grad[half:]
    row = lax.broadcasted_iota(jnp.int32, (TOKENS, SIDE), 0)
    lane = lax.broadcasted_iota(jnp.int32, (TOKENS, SIDE), 1)
    tot = jnp.sum(tot, axis=1, keepdims=True)
    tot_row = jnp.sum(jnp.where(row == lane, tot, 0.0), axis=0, keepdims=True)
    tot_all = jnp.broadcast_to(tot_row, (half, SIDE))
    s_0 = jnp.sum(s_0, axis=1, keepdims=True)
    s_1 = jnp.sum(s_1, axis=1, keepdims=True)
    first, second = by_core(jnp.where(lane == 0, s_0, jnp.where(lane == 1, s_1, 0.0)), core)
    keep_ref[:, D : D + SIDE] = tot_all
    send_ref[:, D : D + SIDE] = tot_all
    keep_ref[:, D + SIDE :] = first
    send_ref[:, D + SIDE :] = second


def latents(others, side, pre_own, resid, gf, w_enc, flipped):
    half = TOKENS // 2
    return call(
        latents_kernel,
        "latents",
        (*others, side, pre_own, resid, gf, w_enc, flipped),
        [((TOKENS, LAT_LOCAL), F32), ((half, RED), F32), ((half, RED), F32)],
        [
            VMEM((PLANE, 2 * OWN, MSG), F32),
            VMEM((TOKENS, LAT_LOCAL), F32),
            VMEM((TOKENS, LAT_LOCAL), BF16),
            VMEM((2 * STEPS + 2, TOKENS, SIDE), F32),
        ],
        flops=4 * 128 * 1024 * D,
    )


def pair_kernel(a_ref, b_ref, p0_ref, p1_ref, p2_ref, p3_ref, packed):
    up = lax.broadcasted_iota(jnp.int32, (8, HALF), 0) >= OWN
    for g in range(PLANE // 2):
        tile = a_ref[8 * g : 8 * g + 8, :] + b_ref[8 * g : 8 * g + 8, :]
        left, right = tile[:, :HALF], tile[:, HALF:]
        packed[2 * g] = jnp.where(up, pltpu.roll(right, OWN, 0), left)
        packed[2 * g + 1] = jnp.where(up, right, pltpu.roll(left, OWN, 0))
    x, z, core = place()
    for d, ref in enumerate((p0_ref, p1_ref, p2_ref, p3_ref)):
        for b in range(4):
            to_x = jnp.where(core == 0, (x + d) % 4, b)
            to_z = jnp.where(core == 0, b, (z + d) % 4)
            ref[b] = packed[to_x * 4 + to_z]


def pair_sum(keep, received):
    return call(
        pair_kernel,
        "pair_sum",
        (keep, received),
        [((4, 8, HALF), F32)] * 4,
        [VMEM((PLANE, 8, HALF), F32)],
    )


def line_sum_kernel(a_ref, b_ref, c_ref, d_ref, p0_ref, p1_ref, p2_ref, p3_ref, total):
    total[...] = (a_ref[...] + b_ref[...]) + (c_ref[...] + d_ref[...])
    x, z, core = place()
    own = jnp.where(core == 0, z, x)
    for e, ref in enumerate((p0_ref, p1_ref, p2_ref, p3_ref)):
        ref[...] = total[(own + e) % 4]


def line_sum(parts):
    return call(
        line_sum_kernel, "line_sum", parts, [((8, HALF), F32)] * 4, [VMEM((4, 8, HALF), F32)]
    )


def plane_kernel(a_ref, b_ref, c_ref, d_ref, out_ref):
    out_ref[...] = (a_ref[...] + b_ref[...]) + (c_ref[...] + d_ref[...])


def plane_sum(parts):
    return call(plane_kernel, "plane_sum", parts, [((8, HALF), F32)])[0]


def result_kernel(
    a_ref, b_ref, c_ref, d_ref, attn_ref, heads_ref, gain_ref, raw_ref, latent_ref, head_ref
):
    total = (a_ref[...] + b_ref[...]) + (c_ref[...] + d_ref[...])
    rest = D - HALF
    g_left, g_right = total[:OWN], total[OWN:, :rest]
    tot_row = total[OWN : OWN + 1, rest : rest + SIDE]
    sums = total[OWN:, rest + SIDE :]
    s_0 = sums[:, 0:1] * (1.0 / D)
    s_1 = sums[:, 1:2] * (1.0 / D)
    head = jnp.zeros((OWN, HEADS_LOCAL), F32)
    lane = lax.broadcasted_iota(jnp.int32, (OWN, HEADS_LOCAL), 1)
    for part, cols in ((g_left, slice(0, HALF)), (g_right, slice(HALF, D))):
        a_0 = attn_ref[:OWN, cols]
        vec = gain_ref[:, cols] * part - (s_0 * a_0 + s_1 * (attn_ref[OWN:, cols] - a_0))
        for h in range(HEADS_LOCAL):
            v = heads_ref[h, OWN:, cols] - heads_ref[h, :OWN, cols]
            dots = jnp.sum(vec * v, axis=1, keepdims=True)
            head = head + jnp.where(lane == h, dots, 0.0)
    head_ref[...] = head * (1.0 / (HEAD_DIM * STEPS))
    row = lax.broadcasted_iota(jnp.int32, (TOKENS, SIDE), 0)
    col = lax.broadcasted_iota(jnp.int32, (TOKENS, SIDE), 1)
    tot = jnp.sum(jnp.where(row == col, tot_row, 0.0), axis=1, keepdims=True)
    latent_ref[...] = raw_ref[...] * (1.0 / (tot * (1.0 / LAT) + EPSILON))


def result(parts, attn, heads, gain, raw):
    return call(
        result_kernel,
        "result",
        (*parts, attn, heads, gain, raw),
        [((TOKENS, LAT_LOCAL), F32), ((OWN, HEADS_LOCAL), F32)],
        final=True,
    )


def over_tp(x, order):
    others = [lax.ppermute(x, "tp", [(i, (i + d) % 4) for i in range(4)]) for d in order]
    return [x] + others


def send(x, stage, d):
    return lax.ppermute(x, "lat", shift(stage, d))


def swap(x):
    return lax.ppermute(x, "lat", CORE_SWAP)


def body(
    z_clean, z_corrupt, resid_clean, resid_corrupt, w_out, post_gain, w_enc, w_dec, cot, active
):
    heads, part = project(z_corrupt, z_clean, w_out)
    part, post_gain, resid_clean, resid_corrupt, w_enc, w_dec, cot, active = lax.optimization_barrier(
        (part, post_gain, resid_clean, resid_corrupt, w_enc, w_dec, cot, active)
    )
    gain = post_gain.reshape(1, D)
    resid = resid_project(resid_corrupt, resid_clean, w_enc)
    *parts, resid = lax.optimization_barrier((*over_tp(part, (3,1,2)), resid))
    attn, msg = norm(parts, resid_corrupt, resid_clean, gain)
    gf = grad_f(cot, w_dec, active)
    parts = [msg] + [send(msg, 0, d) for d in (2, 3, 1)]
    *parts, gf = lax.optimization_barrier((*parts, gf))
    block = line(parts)
    flipped = flip(w_enc)
    blocks = [block] + [send(block, 1, e) for e in (1, 2, 3)]
    first = swap(block)
    blocks[1], flipped, first = lax.optimization_barrier((blocks[1], flipped, first))
    others = [first] + [swap(b) for b in blocks[1:]]
    *blocks, others[1] = lax.optimization_barrier((*blocks, others[1]))
    pre_own, side = own_project(blocks, w_enc)
    raw, keep, give = latents(others, side, pre_own, resid, gf, w_enc, flipped)
    parts = pair_sum(keep, swap(give))
    parts = line_sum([parts[0]] + [send(parts[d], 0, d) for d in (2,1,3)])
    total = plane_sum([parts[0]] + [send(parts[e], 1, e) for e in (2,1,3)])
    return tuple(result(over_tp(total, (3,1,2)), attn, heads, gain, raw))


def solution(mesh):
    placed = (
        P(None, "tp"),
        P(None, "tp"),
        P(),
        P(),
        P("tp", None),
        P(),
        P(None, ("lat", "tp")),
        P(("lat", "tp"), None),
        P(),
        P(None, ("lat", "tp")),
    )
    return jax.shard_map(
        body,
        mesh=mesh,
        in_specs=placed,
        out_specs=(P(None, ("lat", "tp")), P("lat", "tp")),
        check_vma=False,
    )
```
